32 devices in a mesh: pipe: 2 (over core), tensor: 4 (over z), dp: 4 (over y, x).
Axes of the slice: x: 2, y: 2, z: 4, core: 2. Of those that a mesh axis runs over, the one named last changes fastest.
Arguments:
- hidden: bfloat16 [4096, 768], P('dp', 'tensor'), may hold values from -6 to 6
- cotangent: bfloat16 [4096, 768], P('dp', 'tensor'), may hold values from -6 to 6
- segments: int32 [8, 512], P('dp'), may hold values from 0 to 2, never falling along the last dimension, each value on 1 to 384 neighbouring positions
- qkv_weight: bfloat16 [2, 3, 768, 768], P('pipe', None, None, 'tensor'), may hold values from -0.21875 to 0.21875
- qkv_bias: float32 [2, 3, 768], P('pipe', None, 'tensor'), may hold values from -3 to 3
- out_weight: bfloat16 [2, 768, 768], P('pipe', 'tensor'), may hold values from -1.75 to 1.75
- out_bias: float32 [2, 768], P('pipe'), may hold values from -3 to 3
- up_weight: bfloat16 [2, 768, 3072], P('pipe', None, 'tensor'), may hold values from -0.21875 to 0.21875
- up_bias: float32 [2, 3072], P('pipe', 'tensor'), may hold values from -3 to 3
- down_weight: bfloat16 [2, 3072, 768], P('pipe', 'tensor'), may hold values from -0.109375 to 0.109375
- down_bias: float32 [2, 768], P('pipe'), may hold values from -3 to 3
- norm_gain: float32 [2, 2, 768], P('pipe'), may hold values from 0.5 to 1.5
- norm_bias: float32 [2, 2, 768], P('pipe'), may hold values from -3 to 3
Outputs:
- states: bfloat16 [2, 4096, 768], P('pipe', 'dp', 'tensor')
- d_states: float32 [2, 4096, 768], P('pipe', 'dp', 'tensor')
- qkv_weight_grad: float32 [2, 3, 768, 768], P('pipe', None, None, 'tensor')
- qkv_bias_grad: float32 [2, 3, 768], P('pipe', None, 'tensor')
- out_weight_grad: float32 [2, 768, 768], P('pipe', 'tensor')
- out_bias_grad: float32 [2, 768], P('pipe')
- up_weight_grad: float32 [2, 768, 3072], P('pipe', None, 'tensor')
- up_bias_grad: float32 [2, 3072], P('pipe', 'tensor')
- down_weight_grad: float32 [2, 3072, 768], P('pipe', 'tensor')
- down_bias_grad: float32 [2, 768], P('pipe')
- norm_gain_grad: float32 [2, 2, 768], P('pipe')
- norm_bias_grad: float32 [2, 2, 768], P('pipe')
The draws below stay inside these ranges and needn't reach their ends.
Inputs may be any that keep to these rules, and one draw needn't show every extreme that they name: `segments`: each row numbers the documents of one sequence in order, never falling, every number present, each document at most 384 tokens.
All inputs are finite; a program needn't handle non-finite values.
Results may differ from the reference program's by a relative error of at most 0.025.
Values may be sent and summed in bfloat16 or wider, within the bound.
No kernel may reach another device: no remote copies, remote signals or barrier semaphores. Data moves between devices by JAX's collectives and lax.ppermute only.
A program may use at most 192 MiB of HBM per device.

```python
import math
import jax
import jax.numpy as jnp
import numpy as np
from jax import lax

D = 768
HEAD_DIM = 64
FF = 3072
ROT = 16
SEQ_LEN = 512
MICRO = 2
LAYERS = 2
SEQS = 8
TOKENS = 4096
N_TENSOR = 4
N_DP = 4


def steps_of(key, dims, shards, smallest, largest):
    factor_of = 1.0
    for position, parts in shards:
        draws = jax.random.uniform(jax.random.fold_in(jax.random.fold_in(key, 6), position), (parts,), jnp.float32, smallest / len(shards), largest / len(shards))
        factor_of = factor_of * jnp.repeat(jnp.exp(draws), dims[position] // parts).reshape((-1,) + (1,) * (len(dims) - 1 - position))
    return factor_of


def length_profile(number_of, total, most, lean):
    weights = [(1 << 20) // math.isqrt(rank ** lean) + 1 for rank in range(2, number_of + 1)]
    surplus, given = total - most - (number_of - 1), [1] * (number_of - 1)
    while surplus > 0:
        free = [i for i in range(number_of - 1) if given[i] < most]
        pool, left = sum([weights[i] for i in free]), surplus
        for i in free:
            extra = min(most - given[i], max(1, left * weights[i] // pool), surplus)
            given[i] = given[i] + extra
            surplus = surplus - extra
    return np.array([most] + given)


def uneven_parts(stream_key, count, total, most, lean):
    if count == 2:
        one = jax.random.randint(stream_key, (), max(1, total - most), min(most, total - 1) + 1)
        return jnp.stack([one, total - one])
    lengths = jnp.asarray(length_profile(count, total, most, lean), jnp.int32)
    couples = (count - 1) // 2
    source_of, taker = lengths[1:1 + 2 * couples:2], lengths[2:2 + 2 * couples:2]
    room = jnp.minimum(source_of - 1, most - taker)
    moved = jax.random.randint(jax.random.fold_in(stream_key, 1), (couples,), 0, 1 << 20) % (room + 1)
    lengths = lengths.at[1:1 + 2 * couples:2].set(source_of - moved).at[2:2 + 2 * couples:2].set(taker + moved)
    return lengths[jax.random.permutation(jax.random.fold_in(stream_key, 2), count)]


def bell_draw(stream_key, dims, scale, bound, cuts=(), held_as=jnp.bfloat16):
    entries = jax.random.normal(stream_key, dims, jnp.float32) * scale
    if len(cuts) > 0:
        entries = steps_of(stream_key, dims, cuts, -0.22, 0.18) * entries
    return jnp.clip(entries, min=-bound, max=bound).astype(held_as)


def setup_inputs(seed: int = 0) -> dict:
    arg_keys = jax.random.split(jax.random.key(seed), 14)
    hidden = bell_draw(arg_keys[0], (TOKENS, D), 1.0, 6.0, ((0, 4), (1, 4)))
    cotangent = bell_draw(arg_keys[1], (TOKENS, D), 1.0, 6.0, ((0, 4), (1, 4)))
    segments = jax.vmap(lambda own: jnp.searchsorted(jnp.cumsum(uneven_parts(own, 3, SEQ_LEN, 3 * SEQ_LEN // 4, 0)), jnp.arange(SEQ_LEN), side="right"))(jax.random.split(arg_keys[2], SEQS)).reshape((SEQS, SEQ_LEN)).astype(jnp.int32)
    qkv_weight = bell_draw(arg_keys[3], (LAYERS, 3, D, D), D ** -0.5, 0.21875, ((0, 2), (3, 4)))
    qkv_bias = bell_draw(arg_keys[4], (LAYERS, 3, D), 0.3, 3.0, ((0, 2), (2, 4)), jnp.float32)
    out_weight = bell_draw(arg_keys[5], (LAYERS, D, D), (D // 64) ** -0.5, 1.75, ((0, 2), (1, 4)))
    out_bias = bell_draw(arg_keys[6], (LAYERS, D), 0.3, 3.0, ((0, 2),), jnp.float32)
    up_weight = bell_draw(arg_keys[7], (LAYERS, D, FF), D ** -0.5, 0.21875, ((0, 2), (2, 4)))
    up_bias = bell_draw(arg_keys[8], (LAYERS, FF), 0.3, 3.0, ((0, 2), (1, 4)), jnp.float32)
    down_weight = bell_draw(arg_keys[9], (LAYERS, FF, D), FF ** -0.5, 0.109375, ((0, 2), (1, 4)))
    down_bias = bell_draw(arg_keys[10], (LAYERS, D), 0.3, 3.0, ((0, 2),), jnp.float32)
    norm_gain = jnp.clip(1.0 + 0.1 * jax.random.normal(arg_keys[11], (LAYERS, 2, D), jnp.float32), 0.5, 1.5)
    norm_bias = bell_draw(arg_keys[12], (LAYERS, 2, D), 0.3, 3.0, ((0, 2),), jnp.float32)
    return dict(hidden=hidden, cotangent=cotangent, segments=segments, qkv_weight=qkv_weight, qkv_bias=qkv_bias, out_weight=out_weight, out_bias=out_bias, up_weight=up_weight, up_bias=up_bias, down_weight=down_weight, down_bias=down_bias, norm_gain=norm_gain, norm_bias=norm_bias)


@jax.custom_vjp
def low(v):
    return lax.optimization_barrier(v.astype(jnp.bfloat16)).astype(jnp.float32)

@jax.custom_vjp
def low_back(v):
    return v

def low_keep(v):
    return (low(v), None)

def low_pass(kept, grad):
    return (grad,)

def back_keep(v):
    return (v, None)

def back_low(kept, grad):
    return (low(grad),)
low.defvjp(low_keep, low_pass)
low_back.defvjp(back_keep, back_low)
EPSILON = 1e-05
HIGHEST = lax.Precision.HIGHEST

def matmul(left_side, right_side):
    return jnp.dot(left_side, right_side, precision=HIGHEST, preferred_element_type=jnp.float32)

def layer_norm(values, gain_row, shift_row):
    center = values - lax.optimization_barrier(jnp.mean(values, axis=-1, keepdims=True))
    spread = lax.optimization_barrier(jnp.mean(center * center, axis=-1, keepdims=True))
    return center * lax.rsqrt(spread + EPSILON) * gain_row + shift_row

def rotary_tables(seg_rows, rot_dims):
    length = seg_rows.shape[-1]
    before = lax.optimization_barrier(jnp.sum((seg_rows[:, None, :] < seg_rows[:, :, None]).astype(jnp.int32), axis=-1))
    places = jnp.arange(length, dtype=jnp.int32)[None, :] - before
    halves = rot_dims // 2
    freqs = jnp.exp(jnp.arange(halves, dtype=jnp.float32) * (-2.0 * math.log(10000.0) / rot_dims))
    angles = places.astype(jnp.float32)[:, :, None] * freqs
    return (jnp.cos(angles), jnp.sin(angles))

def rotate(values, cosine, sine):
    halves = cosine.shape[-1]
    first = values[..., :halves]
    second = values[..., halves:2 * halves]
    cos_rows = cosine[..., None, :]
    sin_rows = sine[..., None, :]
    return jnp.concatenate([first * cos_rows - second * sin_rows, second * cos_rows + first * sin_rows, values[..., 2 * halves:]], axis=-1)

def one_layer(state, weights, cosine, sine, allowed):
    w_qkv, b_qkv, w_out, b_out, w_up, b_up, w_down, b_down, gains, shifts = weights
    micro_count = allowed.shape[0]
    length = allowed.shape[1]
    rows_all = state.shape[0]
    normed_att = layer_norm(state, gains[0], shifts[0])
    normed_mlp = layer_norm(state, gains[1], shifts[1])
    width = w_out.shape[1]
    local = width // N_TENSOR
    hidden_local = w_up.shape[1] // N_TENSOR
    heads_local = local // HEAD_DIM
    scale = 1.0 / math.sqrt(HEAD_DIM)
    branch = jnp.zeros_like(state)
    for member in range(N_TENSOR):
        column_set = slice(member * local, (member + 1) * local)
        hidden_set = slice(member * hidden_local, (member + 1) * hidden_local)
        att_in = low_back(low(normed_att))
        mlp_in = low_back(low(normed_mlp))
        projected = []
        for which in range(3):
            pre_value = low_back(matmul(att_in, w_qkv[which][:, column_set]) + b_qkv[which][column_set])
            projected.append(pre_value.reshape(micro_count, length, heads_local, HEAD_DIM))
        queries = low_back(low(rotate(projected[0], cosine, sine)))
        key_rows = low_back(low(rotate(projected[1], cosine, sine)))
        value_rows = low_back(low(projected[2]))
        scores = low_back(jnp.einsum('mqhd,mkhd->mhqk', queries, key_rows, precision=HIGHEST) * scale)
        masked = jnp.where(allowed[:, None], scores, -1e+30)
        probs = jax.nn.softmax(masked, axis=-1)
        mixed = jnp.einsum('mhqk,mkhd->mqhd', low(probs), value_rows, precision=HIGHEST).reshape(rows_all, local)
        mixed = low_back(low(mixed))
        activation = low_back(matmul(mlp_in, w_up[:, hidden_set]) + b_up[hidden_set])
        gelu_low = low(jax.nn.gelu(activation, approximate=False))
        partial_sum = matmul(mixed, w_out[column_set, :]) + matmul(gelu_low, w_down[hidden_set, :])
        branch = branch + low(partial_sum)
    branch = low_back(branch)
    return state + branch + b_out + b_down

def group_forward(weights_all, tokens, boundary, cosine, sine, allowed):
    first_layer = jax.tree.map(lambda stacked: stacked[0], weights_all)
    second_layer = jax.tree.map(lambda stacked: stacked[1], weights_all)
    out_first = one_layer(tokens, first_layer, cosine, sine, allowed)
    passed = low_back(low(out_first)) + boundary
    out_second = one_layer(passed, second_layer, cosine, sine, allowed)
    return (out_first, out_second)

def reference(hidden, cotangent, segments, qkv_weight, qkv_bias, out_weight, out_bias, up_weight, up_bias, down_weight, down_bias, norm_gain, norm_bias):
    weights_all = tuple((tensor.astype(jnp.float32) for tensor in (qkv_weight, qkv_bias, out_weight, out_bias, up_weight, up_bias, down_weight, down_bias, norm_gain, norm_bias)))
    group_rows = MICRO * SEQ_LEN
    width = hidden.shape[1]
    tok_groups = hidden.astype(jnp.float32).reshape(N_DP, group_rows, width)
    cot_groups = cotangent.astype(jnp.float32).reshape(N_DP, group_rows, width)
    seg_groups = segments.reshape(N_DP, MICRO, SEQ_LEN)
    positions = jnp.arange(SEQ_LEN, dtype=jnp.int32)

    def step(totals, inputs_one):
        tokens, target, seg_rows = inputs_one
        cosine, sine = rotary_tables(seg_rows, ROT)
        allowed = (seg_rows[:, :, None] == seg_rows[:, None, :]) & (positions[None, :, None] >= positions[None, None, :])
        boundary = jnp.zeros_like(tokens)

        def run(weights_now, tokens_now, boundary_now):
            return group_forward(weights_now, tokens_now, boundary_now, cosine, sine, allowed)
        outputs, pullback = jax.vjp(run, weights_all, tokens, boundary)
        d_weights, d_tokens, d_boundary = pullback((jnp.zeros_like(tokens), target))
        totals = jax.tree.map(lambda earlier, current: earlier + current, totals, d_weights)
        return (totals, (outputs[0], outputs[1], d_tokens, d_boundary))
    start = jax.tree.map(jnp.zeros_like, weights_all)
    grads, results = lax.scan(step, start, (tok_groups, cot_groups, seg_groups))
    out_first, out_second, d_first, d_second = results
    states = jnp.stack([out_first.reshape(-1, width), out_second.reshape(-1, width)]).astype(jnp.bfloat16)
    d_states = jnp.stack([d_first.reshape(-1, width), d_second.reshape(-1, width)])
    return (states, d_states, grads[0], grads[1], grads[2], grads[3], grads[4], grads[5], grads[6], grads[7], grads[8], grads[9])
```

```python
from functools import partial
import math

import jax
import jax.numpy as jnp
from jax import lax
from jax.sharding import PartitionSpec as P

HEAD_DIM = 64
ROT = 16
SEQ_LEN = 512
EPSILON = 1e-05
LOW = jnp.bfloat16
FULL = jnp.float32


def swap(value):
    return lax.ppermute(value, "pipe", [(0, 1), (1, 0)])


def partner(value, axis, flip):
    count = lax.axis_size(axis)
    return lax.ppermute(value, axis, [(source, source ^ flip) for source in range(count)])


def pair_sum(terms):
    while len(terms) > 1:
        terms = [first + second for first, second in zip(terms[0::2], terms[1::2])]
    return terms[0]


def scatter_sum(piece_of, axis):
    me = lax.axis_index(axis)
    terms = [piece_of(me).astype(FULL)]
    for flip in range(1, lax.axis_size(axis)):
        terms.append(partner(piece_of(me ^ flip), axis, flip).astype(FULL))
    return pair_sum(terms)


def gather_rows(value, axis):
    me = lax.axis_index(axis)
    blocks = [value]
    for flip in range(1, lax.axis_size(axis)):
        blocks.append(partner(value, axis, flip))
    stacked = jnp.stack(blocks)
    ordered = [
        lax.dynamic_index_in_dim(stacked, place ^ me, 0, keepdims=False)
        for place in range(lax.axis_size(axis))
    ]
    return jnp.concatenate(ordered, axis=0)


def whole_sum(value, axis):
    terms = [value]
    for flip in range(1, lax.axis_size(axis)):
        terms.append(partner(value, axis, flip))
    return pair_sum(terms)


def rotary_tables(seg_row):
    length = seg_row.shape[-1]
    before = jnp.sum((seg_row[None, :] < seg_row[:, None]).astype(jnp.int32), axis=-1)
    places = jnp.arange(length, dtype=jnp.int32) - before
    halves = ROT // 2
    freqs = jnp.exp(jnp.arange(halves, dtype=FULL) * (-2.0 * math.log(10000.0) / ROT))
    angles = places.astype(FULL)[:, None] * freqs
    return (jnp.cos(angles), jnp.sin(angles))


def rotate(values, cosine, sine):
    halves = cosine.shape[-1]
    first = values[..., :halves]
    second = values[..., halves : 2 * halves]
    cos_rows = cosine[..., None, :]
    sin_rows = sine[..., None, :]
    return jnp.concatenate(
        [
            first * cos_rows - second * sin_rows,
            second * cos_rows + first * sin_rows,
            values[..., 2 * halves :],
        ],
        axis=-1,
    )


def body(
    hidden,
    cotangent,
    segments,
    qkv_weight,
    qkv_bias,
    out_weight,
    out_bias,
    up_weight,
    up_bias,
    down_weight,
    down_bias,
    norm_gain,
    norm_bias,
):
    section = lax.axis_index("pipe")
    member = lax.axis_index("tensor")
    members = lax.axis_size("tensor")
    first_core = section == 0
    length = SEQ_LEN
    local = qkv_weight.shape[3]
    heads = local // HEAD_DIM
    width = qkv_weight.shape[2]
    units = up_weight.shape[2]
    scale = 1.0 / math.sqrt(HEAD_DIM)

    own_rows = lambda rows: lax.dynamic_slice_in_dim(rows, section * length, length, 0)
    state_in = lax.all_gather(own_rows(hidden), "tensor", axis=1, tiled=True)
    target = lax.all_gather(own_rows(cotangent), "tensor", axis=1, tiled=True)
    seg_row = lax.dynamic_index_in_dim(segments, section, 0, keepdims=False)

    def both(value):
        other = swap(value)
        return (jnp.where(first_core, value, other), jnp.where(first_core, other, value))

    vectors = [qkv_bias, out_bias, up_bias, down_bias, norm_gain, norm_bias]
    packed = both(jnp.concatenate([vector.reshape(-1) for vector in vectors]))
    layers = [[], []]
    for weight in (qkv_weight, out_weight, up_weight, down_weight):
        for layer, value in enumerate(both(weight[0])):
            layers[layer].append(value)
    for layer in range(2):
        start = 0
        for vector in vectors:
            piece = packed[layer][start : start + vector.size].reshape(vector.shape[1:])
            layers[layer].append(piece)
            start += vector.size

    cosine, sine = rotary_tables(seg_row)
    positions = jnp.arange(length, dtype=jnp.int32)
    allowed = (seg_row[:, None] == seg_row[None, :]) & (positions[:, None] >= positions[None, :])

    def masked_scores(queries, key_rows):
        scores = jnp.einsum("qhd,khd->hqk", queries, key_rows, preferred_element_type=FULL)
        return jnp.where(allowed[None], scores * scale, -1e30)

    def forward(state, weights):
        w_qkv, w_out, w_up, w_down, b_qkv, b_out, b_up, b_down, gains, shifts = weights
        center = state - jnp.mean(state, axis=-1, keepdims=True)
        spread = lax.rsqrt(jnp.mean(center * center, axis=-1, keepdims=True) + EPSILON)
        unit = center * spread
        att_low = (unit * gains[0] + shifts[0]).astype(LOW)
        mlp_low = (unit * gains[1] + shifts[1]).astype(LOW)
        projected = (
            jnp.einsum("td,cde->cte", att_low, w_qkv, preferred_element_type=FULL)
            + b_qkv[:, None, :]
        ).reshape(3, length, heads, HEAD_DIM)
        queries = rotate(projected[0], cosine, sine).astype(LOW)
        key_rows = rotate(projected[1], cosine, sine).astype(LOW)
        value_rows = projected[2].astype(LOW)
        masked = masked_scores(queries, key_rows)
        peak = jnp.max(masked, axis=-1, keepdims=True)
        exponent = jnp.exp(masked - peak)
        totals = jnp.sum(exponent, axis=-1, keepdims=True)
        log_total = peak + jnp.log(totals)
        probs_low = (exponent / totals).astype(LOW)
        mixed = jnp.einsum("hqk,khd->qhd", probs_low, value_rows, preferred_element_type=FULL)
        mixed = mixed.reshape(length, local).astype(LOW)
        activation = jnp.dot(mlp_low, w_up, preferred_element_type=FULL) + b_up
        gelu_low = jax.nn.gelu(activation, approximate=False).astype(LOW)
        branch = jnp.dot(mixed, w_out, preferred_element_type=FULL) + jnp.dot(
            gelu_low, w_down, preferred_element_type=FULL
        )
        saved = (
            unit,
            spread,
            att_low,
            mlp_low,
            queries,
            key_rows,
            value_rows,
            log_total,
            mixed,
            activation,
            gelu_low,
        )
        return branch.astype(LOW), saved

    def backward(grad_low, weights, saved):
        w_qkv, w_out, w_up, w_down, b_qkv, b_out, b_up, b_down, gains, shifts = weights
        (
            unit,
            spread,
            att_low,
            mlp_low,
            queries,
            key_rows,
            value_rows,
            log_total,
            mixed,
            activation,
            gelu_low,
        ) = saved
        g_down = jnp.einsum("tf,td->fd", gelu_low, grad_low, preferred_element_type=FULL)
        g_out = jnp.einsum("te,td->ed", mixed, grad_low, preferred_element_type=FULL)
        d_gelu = jnp.einsum("td,fd->tf", grad_low, w_down, preferred_element_type=FULL)
        gelu_slope = 0.5 * (1.0 + lax.erf(activation * math.sqrt(0.5))) + activation * (
            jnp.exp(-0.5 * activation * activation) * (1.0 / math.sqrt(2.0 * math.pi))
        )
        d_act = (d_gelu * gelu_slope).astype(LOW)
        d_mlp = jnp.einsum("tf,df->td", d_act, w_up, preferred_element_type=FULL)
        g_up = jnp.einsum("td,tf->df", mlp_low, d_act, preferred_element_type=FULL)
        d_mixed = jnp.einsum("td,ed->te", grad_low, w_out, preferred_element_type=FULL)
        d_mixed = d_mixed.astype(LOW).reshape(length, heads, HEAD_DIM)
        probs = jnp.exp(masked_scores(queries, key_rows) - log_total)
        d_probs = jnp.einsum("qhd,khd->hqk", d_mixed, value_rows, preferred_element_type=FULL)
        middle = jnp.sum(d_probs * probs, axis=-1, keepdims=True)
        d_scores = (probs * (d_probs - middle)).astype(LOW)
        d_queries = jnp.einsum("hqk,khd->qhd", d_scores, key_rows, preferred_element_type=FULL)
        d_keys = jnp.einsum("hqk,qhd->khd", d_scores, queries, preferred_element_type=FULL)
        d_values = jnp.einsum(
            "hqk,qhd->khd", probs.astype(LOW), d_mixed, preferred_element_type=FULL
        )
        d_proj = (
            jnp.stack(
                [
                    rotate(d_queries * scale, cosine, -sine),
                    rotate(d_keys * scale, cosine, -sine),
                    d_values,
                ]
            )
            .astype(LOW)
            .reshape(3, length, local)
        )
        d_att = jnp.einsum("cte,cde->td", d_proj, w_qkv, preferred_element_type=FULL)
        g_qkv = jnp.einsum("td,cte->cde", att_low, d_proj, preferred_element_type=FULL)
        d_unit = d_att * gains[0] + d_mlp * gains[1]
        norm_rows = jnp.stack(
            [
                jnp.sum(d_att * unit, axis=0),
                jnp.sum(d_mlp * unit, axis=0),
                jnp.sum(d_att, axis=0),
                jnp.sum(d_mlp, axis=0),
            ]
        )
        bias_rows = jnp.stack(
            [
                jnp.sum(grad_low.astype(FULL), axis=0),
                jnp.sum(d_act.astype(FULL), axis=0),
                jnp.pad(
                    jnp.sum(d_proj.astype(FULL), axis=1).reshape(-1), (0, width - 3 * local)
                ),
            ]
        )
        grads = (g_down, g_out, g_up, g_qkv.reshape(3 * width, local))
        return d_unit, norm_rows, bias_rows, grads

    def half_share(gradient):
        gradient = gradient.astype(LOW)
        half = gradient.shape[0] // 2
        kept = lax.dynamic_slice_in_dim(gradient, section * half, half, 0)
        sent = lax.dynamic_slice_in_dim(gradient, (1 - section) * half, half, 0)
        total = (kept.astype(FULL) + swap(sent).astype(FULL)).astype(LOW)
        groups = lax.axis_size("dp")
        if groups > 4:
            share = lax.psum_scatter(total, "dp", scatter_dimension=0, tiled=True)
            return lax.all_gather(share, "dp", axis=0, tiled=True)
        rows = half // groups
        share = scatter_sum(
            lambda place: lax.dynamic_slice_in_dim(total, place * rows, rows, 0), "dp"
        ).astype(LOW)
        return gather_rows(share, "dp")

    rows_part = length // members
    token_part = lambda values: scatter_sum(
        lambda place: lax.dynamic_slice_in_dim(values, place * rows_part, rows_part, 0), "tensor"
    )
    feature_part = lambda values: scatter_sum(
        lambda place: lax.dynamic_slice_in_dim(values, place * local, local, 1), "tensor"
    )
    own_features = lambda values: lax.dynamic_slice_in_dim(values, member * local, local, 1)
    own_tokens = lambda values: lax.dynamic_slice_in_dim(values, member * rows_part, rows_part, 0)

    first, second = layers
    branch0, saved0 = forward(state_in.astype(FULL), first)
    out0 = own_tokens(state_in).astype(FULL) + token_part(branch0) + first[5] + first[7]
    state1 = lax.all_gather(out0.astype(LOW), "tensor", axis=0, tiled=True)
    branch1, saved1 = forward(state1.astype(FULL), second)
    out1 = (
        own_features(state1).astype(FULL)
        + feature_part(branch1)
        + own_features((second[5] + second[7])[None])
    )

    def moments(d_unit, unit):
        return jnp.stack([jnp.mean(d_unit, axis=-1), jnp.mean(d_unit * unit, axis=-1)], axis=-1)

    d_unit1, norm_rows1, bias_rows1, grads1 = backward(target, second, saved1)
    d_sum1 = token_part(d_unit1.astype(LOW))
    unit1 = own_tokens(saved1[0])
    part1 = moments(d_sum1, unit1)
    d_in1 = own_tokens(target).astype(FULL) + own_tokens(saved1[1]) * (
        d_sum1 - part1[:, :1] - unit1 * part1[:, 1:]
    )
    grad0 = lax.all_gather(d_in1.astype(LOW), "tensor", axis=0, tiled=True)
    shares1 = [half_share(gradient) for gradient in grads1]

    d_unit0, norm_rows0, bias_rows0, grads0 = backward(grad0, first, saved0)
    shares0 = [half_share(gradient) for gradient in grads0]
    d_low0 = d_unit0.astype(LOW)
    part0 = whole_sum(moments(d_low0.astype(FULL), saved0[0]), "tensor")
    d_in0 = own_features(grad0).astype(FULL) + saved0[1] * (
        feature_part(d_low0) - part0[:, :1] - own_features(saved0[0]) * part0[:, 1:]
    )

    norm_rows = whole_sum(jnp.concatenate([norm_rows0, norm_rows1]), "tensor")
    small = jnp.concatenate([norm_rows, bias_rows0, bias_rows1])
    small = small + swap(small)
    if lax.axis_size("dp") > 4:
        small = lax.psum(small, "dp")
    else:
        small = whole_sum(small, "dp")
    norm_rows = jnp.where(first_core, small[0:4], small[4:8])
    bias_rows = jnp.where(first_core, small[8:11], small[11:14])

    def by_layer(low_value, high_value):
        mine = jnp.where(first_core, low_value, high_value)
        other = swap(jnp.where(first_core, high_value, low_value))
        return jnp.concatenate(
            [jnp.where(first_core, mine, other), jnp.where(first_core, other, mine)], axis=0
        )

    states_out = by_layer(own_features(state1), out1.astype(LOW))[None]
    d_states_out = by_layer(d_in0, own_features(grad0).astype(FULL))[None]
    g_down, g_out, g_up, g_qkv = [
        by_layer(low_half, high_half).astype(FULL)
        for low_half, high_half in zip(shares0, shares1)
    ]
    return (
        states_out,
        d_states_out,
        g_qkv.reshape(qkv_weight.shape),
        bias_rows[2, : 3 * local].reshape(qkv_bias.shape),
        g_out.reshape(out_weight.shape),
        bias_rows[0][None],
        g_up.reshape(up_weight.shape),
        bias_rows[1][None],
        g_down.reshape(down_weight.shape),
        bias_rows[0][None],
        norm_rows[0:2][None],
        norm_rows[2:4][None],
    )


def solution(mesh):
    in_specs = (
        P("dp", "tensor"),
        P("dp", "tensor"),
        P("dp", None),
        P("pipe", None, None, "tensor"),
        P("pipe", None, "tensor"),
        P("pipe", "tensor", None),
        P("pipe", None),
        P("pipe", None, "tensor"),
        P("pipe", "tensor"),
        P("pipe", "tensor", None),
        P("pipe", None),
        P("pipe", None, None),
        P("pipe", None, None),
    )
    out_specs = (
        P("pipe", "dp", "tensor"),
        P("pipe", "dp", "tensor"),
        P("pipe", None, None, "tensor"),
        P("pipe", None, "tensor"),
        P("pipe", "tensor", None),
        P("pipe", None),
        P("pipe", None, "tensor"),
        P("pipe", "tensor"),
        P("pipe", "tensor", None),
        P("pipe", None),
        P("pipe", None, None),
        P("pipe", None, None),
    )
    return jax.shard_map(body, mesh=mesh, in_specs=in_specs, out_specs=out_specs, check_vma=False)
```

```python
from functools import partial
import math

import jax
import jax.numpy as jnp
from jax import lax
from jax.sharding import PartitionSpec as P

HEAD_DIM = 64
ROT = 16
SEQ_LEN = 512
EPSILON = 1e-05
LOW = jnp.bfloat16
FULL = jnp.float32


def swap(value):
    return lax.ppermute(value, "pipe", [(0, 1), (1, 0)])


def partner(value, axis, flip):
    count = lax.axis_size(axis)
    return lax.ppermute(value, axis, [(source, source ^ flip) for source in range(count)])


def pair_sum(terms):
    while len(terms) > 1:
        terms = [first + second for first, second in zip(terms[0::2], terms[1::2])]
    return terms[0]


def scatter_sum(piece_of, axis):
    me = lax.axis_index(axis)
    terms = [piece_of(me).astype(FULL)]
    for flip in range(1, lax.axis_size(axis)):
        terms.append(partner(piece_of(me ^ flip), axis, flip).astype(FULL))
    return pair_sum(terms)


def gather_blocks(value, axis, dim):
    me = lax.axis_index(axis)
    blocks = [value]
    for flip in range(1, lax.axis_size(axis)):
        blocks.append(partner(value, axis, flip))
    stacked = jnp.stack(blocks)
    ordered = [
        lax.dynamic_index_in_dim(stacked, place ^ me, 0, keepdims=False)
        for place in range(lax.axis_size(axis))
    ]
    return jnp.concatenate(ordered, axis=dim)


def whole_sum(value, axis):
    terms = [value]
    for flip in range(1, lax.axis_size(axis)):
        terms.append(partner(value, axis, flip))
    return pair_sum(terms)


def direct_sum(total, axis):
    count = lax.axis_size(axis)
    if count > 4:
        share = lax.psum_scatter(total, axis, scatter_dimension=0, tiled=True)
        return lax.all_gather(share, axis, axis=0, tiled=True)
    rows = total.shape[0] // count
    share = scatter_sum(
        lambda place: lax.dynamic_slice_in_dim(total, place * rows, rows, 0), axis
    )
    return gather_blocks(share.astype(LOW), axis, 0)


def halve(total, axis, flip):
    side = (lax.axis_index(axis) // flip) % 2
    half = total.shape[0] // 2
    kept = lax.dynamic_slice_in_dim(total, side * half, half, 0)
    sent = lax.dynamic_slice_in_dim(total, (1 - side) * half, half, 0)
    return (kept.astype(FULL) + partner(sent, axis, flip).astype(FULL)).astype(LOW)


def double(share, axis, flip):
    upper = ((lax.axis_index(axis) // flip) % 2) == 1
    other = partner(share, axis, flip)
    return jnp.concatenate(
        [jnp.where(upper, other, share), jnp.where(upper, share, other)], axis=0
    )


def tie(*values):
    return lax.optimization_barrier(values)


def rotary_tables(seg_row):
    length = seg_row.shape[-1]
    before = jnp.sum((seg_row[None, :] < seg_row[:, None]).astype(jnp.int32), axis=-1)
    places = jnp.arange(length, dtype=jnp.int32) - before
    halves = ROT // 2
    freqs = jnp.exp(jnp.arange(halves, dtype=FULL) * (-2.0 * math.log(10000.0) / ROT))
    angles = places.astype(FULL)[:, None] * freqs
    return (jnp.cos(angles), jnp.sin(angles))


def rotate(values, cosine, sine):
    halves = cosine.shape[-1]
    first = values[..., :halves]
    second = values[..., halves : 2 * halves]
    cos_rows = cosine[..., None, :]
    sin_rows = sine[..., None, :]
    return jnp.concatenate(
        [
            first * cos_rows - second * sin_rows,
            second * cos_rows + first * sin_rows,
            values[..., 2 * halves :],
        ],
        axis=-1,
    )


def body(
    hidden,
    cotangent,
    segments,
    qkv_weight,
    qkv_bias,
    out_weight,
    out_bias,
    up_weight,
    up_bias,
    down_weight,
    down_bias,
    norm_gain,
    norm_bias,
):
    section = lax.axis_index("pipe")
    member = lax.axis_index("tensor")
    members = lax.axis_size("tensor")
    first_core = section == 0
    length = SEQ_LEN
    local = qkv_weight.shape[3]
    heads = local // HEAD_DIM
    width = qkv_weight.shape[2]
    units = up_weight.shape[2]
    scale = 1.0 / math.sqrt(HEAD_DIM)

    own_rows = lambda rows: lax.dynamic_slice_in_dim(rows, section * length, length, 0)
    state_in = lax.all_gather(own_rows(hidden), "tensor", axis=1, tiled=True)
    target_part, state_in = tie(own_rows(cotangent), state_in)
    target = gather_blocks(target_part, "tensor", 1)
    seg_row = lax.dynamic_index_in_dim(segments, section, 0, keepdims=False)

    def both(value):
        other = swap(value)
        return (jnp.where(first_core, value, other), jnp.where(first_core, other, value))

    vectors = [qkv_bias, out_bias, up_bias, down_bias, norm_gain, norm_bias]
    packed = both(jnp.concatenate([vector.reshape(-1) for vector in vectors]))
    layers = [[], []]
    for weight in (qkv_weight, out_weight, up_weight, down_weight):
        for layer, value in enumerate(both(weight[0])):
            layers[layer].append(value)
    for layer in range(2):
        start = 0
        for vector in vectors:
            piece = packed[layer][start : start + vector.size].reshape(vector.shape[1:])
            layers[layer].append(piece)
            start += vector.size

    cosine, sine = rotary_tables(seg_row)
    positions = jnp.arange(length, dtype=jnp.int32)
    allowed = (seg_row[:, None] == seg_row[None, :]) & (positions[:, None] >= positions[None, :])

    def masked_scores(queries, key_rows):
        scores = jnp.einsum("qhd,khd->hqk", queries, key_rows, preferred_element_type=FULL)
        return jnp.where(allowed[None], scores * scale, -1e30)

    def forward(state, weights):
        w_qkv, w_out, w_up, w_down, b_qkv, b_out, b_up, b_down, gains, shifts = weights
        center = state - jnp.mean(state, axis=-1, keepdims=True)
        spread = lax.rsqrt(jnp.mean(center * center, axis=-1, keepdims=True) + EPSILON)
        unit = center * spread
        att_low = (unit * gains[0] + shifts[0]).astype(LOW)
        mlp_low = (unit * gains[1] + shifts[1]).astype(LOW)
        projected = (
            jnp.einsum("td,cde->cte", att_low, w_qkv, preferred_element_type=FULL)
            + b_qkv[:, None, :]
        ).reshape(3, length, heads, HEAD_DIM)
        queries = rotate(projected[0], cosine, sine).astype(LOW)
        key_rows = rotate(projected[1], cosine, sine).astype(LOW)
        value_rows = projected[2].astype(LOW)
        masked = masked_scores(queries, key_rows)
        peak = jnp.max(masked, axis=-1, keepdims=True)
        exponent = jnp.exp(masked - peak)
        totals = jnp.sum(exponent, axis=-1, keepdims=True)
        log_total = peak + jnp.log(totals)
        probs_low = (exponent / totals).astype(LOW)
        mixed = jnp.einsum("hqk,khd->qhd", probs_low, value_rows, preferred_element_type=FULL)
        mixed = mixed.reshape(length, local).astype(LOW)
        activation = jnp.dot(mlp_low, w_up, preferred_element_type=FULL) + b_up
        gelu_low = jax.nn.gelu(activation, approximate=False).astype(LOW)
        branch = jnp.dot(mixed, w_out, preferred_element_type=FULL) + jnp.dot(
            gelu_low, w_down, preferred_element_type=FULL
        )
        saved = (
            unit,
            spread,
            att_low,
            mlp_low,
            queries,
            key_rows,
            value_rows,
            log_total,
            mixed,
            activation,
            gelu_low,
        )
        return branch.astype(LOW), saved

    def backward(grad_low, weights, saved, along):
        w_qkv, w_out, w_up, w_down, b_qkv, b_out, b_up, b_down, gains, shifts = weights
        (
            unit,
            spread,
            att_low,
            mlp_low,
            queries,
            key_rows,
            value_rows,
            log_total,
            mixed,
            activation,
            gelu_low,
        ) = saved
        g_down = jnp.einsum("tf,td->fd", gelu_low, grad_low, preferred_element_type=FULL)
        g_out = jnp.einsum("te,td->ed", mixed, grad_low, preferred_element_type=FULL)
        early = jnp.concatenate([g_down.astype(LOW), g_out.astype(LOW)])
        d_gelu = jnp.einsum("td,fd->tf", grad_low, w_down, preferred_element_type=FULL)
        gelu_slope = 0.5 * (1.0 + lax.erf(activation * math.sqrt(0.5))) + activation * (
            jnp.exp(-0.5 * activation * activation) * (1.0 / math.sqrt(2.0 * math.pi))
        )
        d_act = (d_gelu * gelu_slope).astype(LOW)
        g_up = jnp.einsum("td,tf->df", mlp_low, d_act, preferred_element_type=FULL)
        d_mixed = jnp.einsum("td,ed->te", grad_low, w_out, preferred_element_type=FULL)
        d_mixed = d_mixed.astype(LOW).reshape(length, heads, HEAD_DIM)
        probs = jnp.exp(masked_scores(queries, key_rows) - log_total)
        d_probs = jnp.einsum("qhd,khd->hqk", d_mixed, value_rows, preferred_element_type=FULL)
        middle = jnp.sum(d_probs * probs, axis=-1, keepdims=True)
        d_scores = (probs * (d_probs - middle)).astype(LOW)
        d_queries = jnp.einsum("hqk,khd->qhd", d_scores, key_rows, preferred_element_type=FULL)
        d_keys = jnp.einsum("hqk,qhd->khd", d_scores, queries, preferred_element_type=FULL)
        d_values = jnp.einsum(
            "hqk,qhd->khd", probs.astype(LOW), d_mixed, preferred_element_type=FULL
        )
        d_proj = (
            jnp.stack(
                [
                    rotate(d_queries * scale, cosine, -sine),
                    rotate(d_keys * scale, cosine, -sine),
                    d_values,
                ]
            )
            .astype(LOW)
            .reshape(3, length, local)
        )
        d_proj = along(0, d_proj)
        d_att = jnp.einsum("cte,cde->td", d_proj, w_qkv, preferred_element_type=FULL)
        d_mlp = jnp.einsum("tf,df->td", d_act, w_up, preferred_element_type=FULL)
        g_qkv = jnp.einsum("cte,td->ced", d_proj, att_low, preferred_element_type=FULL)
        late = jnp.concatenate([g_up.astype(LOW), g_qkv.reshape(3 * local, width).astype(LOW)])
        d_unit = d_att * gains[0] + d_mlp * gains[1]
        small = jnp.stack(
            [
                jnp.sum(d_att * unit, axis=0),
                jnp.sum(d_mlp * unit, axis=0),
                jnp.sum(d_att, axis=0),
                jnp.sum(d_mlp, axis=0),
                jnp.sum(grad_low.astype(FULL), axis=0),
                jnp.sum(d_act.astype(FULL), axis=0),
                jnp.pad(
                    jnp.sum(d_proj.astype(FULL), axis=1).reshape(-1), (0, width - 3 * local)
                ),
                jnp.zeros(width, FULL),
            ]
        )
        return d_unit, small, early, late

    def halves(gradient):
        half = gradient.shape[0] // 2
        kept = lax.dynamic_slice_in_dim(gradient, section * half, half, 0)
        sent = lax.dynamic_slice_in_dim(gradient, (1 - section) * half, half, 0)
        return kept, sent

    def core_sum(kept, sent):
        return (kept.astype(FULL) + swap(sent).astype(FULL)).astype(LOW)

    rows_part = length // members
    token_part = lambda values: scatter_sum(
        lambda place: lax.dynamic_slice_in_dim(values, place * rows_part, rows_part, 0), "tensor"
    )
    feature_part = lambda values: scatter_sum(
        lambda place: lax.dynamic_slice_in_dim(values, place * local, local, 1), "tensor"
    )
    own_features = lambda values: lax.dynamic_slice_in_dim(values, member * local, local, 1)
    own_tokens = lambda values: lax.dynamic_slice_in_dim(values, member * rows_part, rows_part, 0)

    first, second = layers
    branch0, saved0 = forward(state_in.astype(FULL), first)
    out0 = own_tokens(state_in).astype(FULL) + token_part(branch0) + first[5] + first[7]
    state1 = lax.all_gather(out0.astype(LOW), "tensor", axis=0, tiled=True)
    branch1, saved1 = forward(state1.astype(FULL), second)
    out1 = (
        own_features(state1).astype(FULL)
        + feature_part(branch1)
        + own_features((second[5] + second[7])[None])
    )

    def moments(d_unit, unit):
        return jnp.stack([jnp.mean(d_unit, axis=-1), jnp.mean(d_unit * unit, axis=-1)], axis=-1)

    groups = lax.axis_size("dp")
    flips = [1 << step for step in range(groups.bit_length() - 1)]
    d_unit1, small1, early1, late1 = backward(target, second, saved1, lambda stage, value: value)
    d_low1 = d_unit1.astype(LOW)
    d_sum1 = token_part(d_low1)
    kept1, sent1 = [jnp.concatenate(parts) for parts in zip(halves(early1), halves(late1))]
    total1 = core_sum(kept1, sent1)
    unit1 = own_tokens(saved1[0])
    part1 = moments(d_sum1, unit1)
    d_in1 = own_tokens(target).astype(FULL) + own_tokens(saved1[1]) * (
        d_sum1 - part1[:, :1] - unit1 * part1[:, 1:]
    )
    d_in1_low, total1 = tie(d_in1.astype(LOW), total1)
    lower1, upper1 = jnp.split(total1, 2)
    lower1, upper1 = halve(lower1, "dp", flips[0]), halve(upper1, "dp", flips[-1])
    grad0 = lax.all_gather(d_in1_low, "tensor", axis=0, tiled=True)
    grad0, lower1, upper1 = tie(grad0, lower1, upper1)
    for flip in flips[1:]:
        lower1 = halve(lower1, "dp", flip)
    for flip in flips[-2::-1]:
        upper1 = halve(upper1, "dp", flip)
    held = [lower1, upper1]

    def along(stage, value):
        value, held[0], held[1] = tie(value, *held)
        return value

    d_unit0, small0, early0, late0 = backward(grad0, first, saved0, along)
    lower1, upper1 = held
    for flip in flips[::-1]:
        lower1 = double(lower1, "dp", flip)
    for flip in flips:
        upper1 = double(upper1, "dp", flip)
    whole1 = jnp.concatenate([lower1, upper1])

    early_half = direct_sum(core_sum(*halves(early0)), "dp")
    small = jnp.concatenate([small0, small1]).astype(LOW)
    small = jnp.concatenate([small, jnp.zeros_like(small)])
    late_half = direct_sum(
        core_sum(*[jnp.concatenate([part, small]) for part in halves(late0)]), "dp"
    )
    late_rows = late_half.shape[0] - small.shape[0]
    late_half, small = late_half[:late_rows], late_half[late_rows:].astype(FULL)
    small = jnp.where(first_core, small[0:8], small[8:16])
    norm_rows = whole_sum(small[0:4], "tensor")

    d_low0 = d_unit0.astype(LOW)
    part0 = moments(d_low0.astype(FULL), saved0[0]).astype(LOW)
    d_sum0 = scatter_sum(
        lambda place: jnp.concatenate(
            [lax.dynamic_slice_in_dim(d_low0, place * local, local, 1), part0], axis=1
        ),
        "tensor",
    )
    part0 = d_sum0[:, local:]
    d_in0 = own_features(grad0).astype(FULL) + saved0[1] * (
        d_sum0[:, :local] - part0[:, :1] - own_features(saved0[0]) * part0[:, 1:]
    )

    def by_layer(low_value, high_value):
        mine = jnp.where(first_core, low_value, high_value)
        other = swap(jnp.where(first_core, high_value, low_value))
        return jnp.concatenate(
            [jnp.where(first_core, mine, other), jnp.where(first_core, other, mine)], axis=0
        )

    states_out = by_layer(own_features(state1), out1.astype(LOW))[None]
    d_states_out = by_layer(d_in0, own_features(grad0).astype(FULL))[None]
    early_rows = early_half.shape[0]
    early = by_layer(early_half, whole1[:early_rows]).astype(FULL)
    late = by_layer(late_half, whole1[early_rows:]).astype(FULL)
    g_down, g_out = early[:units], early[units:]
    g_up, g_qkv = late[:width], late[width:]
    return (
        states_out,
        d_states_out,
        g_qkv.reshape(3, local, width).swapaxes(1, 2)[None],
        small[6, : 3 * local].reshape(qkv_bias.shape),
        g_out[None],
        small[4][None],
        g_up[None],
        small[5][None],
        g_down[None],
        small[4][None],
        norm_rows[0:2][None],
        norm_rows[2:4][None],
    )


def solution(mesh):
    in_specs = (
        P("dp", "tensor"),
        P("dp", "tensor"),
        P("dp", None),
        P("pipe", None, None, "tensor"),
        P("pipe", None, "tensor"),
        P("pipe", "tensor", None),
        P("pipe", None),
        P("pipe", None, "tensor"),
        P("pipe", "tensor"),
        P("pipe", "tensor", None),
        P("pipe", None),
        P("pipe", None, None),
        P("pipe", None, None),
    )
    out_specs = (
        P("pipe", "dp", "tensor"),
        P("pipe", "dp", "tensor"),
        P("pipe", None, None, "tensor"),
        P("pipe", None, "tensor"),
        P("pipe", "tensor", None),
        P("pipe", None),
        P("pipe", None, "tensor"),
        P("pipe", "tensor"),
        P("pipe", "tensor", None),
        P("pipe", None),
        P("pipe", None, None),
        P("pipe", None, None),
    )
    return jax.shard_map(body, mesh=mesh, in_specs=in_specs, out_specs=out_specs, check_vma=False)
```

```python
from functools import partial
import math

import jax
import jax.numpy as jnp
from jax import lax
from jax.experimental import pallas as pl
from jax.experimental.pallas import tpu as pltpu
from jax.sharding import PartitionSpec as P

HEAD_DIM = 64
ROT = 16
SEQ_LEN = 512
EPSILON = 1e-05
LOW = jnp.bfloat16
FULL = jnp.float32


def swap(value):
    return lax.ppermute(value, "pipe", [(0, 1), (1, 0)])


def partner(value, axis, flip):
    count = lax.axis_size(axis)
    return lax.ppermute(value, axis, [(source, source ^ flip) for source in range(count)])


def pair_sum(terms):
    while len(terms) > 1:
        terms = [first + second for first, second in zip(terms[0::2], terms[1::2])]
    return terms[0]


def scattered(piece_of, axis, me):
    terms = [piece_of(me)]
    for flip in range(1, lax.axis_size(axis)):
        terms.append(partner(piece_of(me ^ flip), axis, flip))
    return terms


def total_of(terms):
    return pair_sum([term.astype(FULL) for term in terms])


def received(value, axis):
    return [value] + [partner(value, axis, flip) for flip in range(1, lax.axis_size(axis))]


def tie(*values):
    return lax.optimization_barrier(values)


def rows_kernel(me, *refs):
    blocks, out, sems = refs[:-2], refs[-2], refs[-1]
    rows = blocks[0].shape[0]
    copies = []
    for flip, block in enumerate(blocks):
        start = pl.multiple_of((me[0] ^ flip) * rows, 16)
        copies.append(
            pltpu.make_async_copy(block, out.at[pl.ds(start, rows), :], sems.at[flip])
        )
    for copy in copies:
        copy.start()
    for copy in copies:
        copy.wait()


def columns_kernel(me, *refs):
    blocks, out = refs[:-1], refs[-1]
    wide = blocks[0].shape[1]
    for place in range(len(blocks)):
        for flip, block in enumerate(blocks):

            @pl.when(me[0] == place ^ flip)
            def _():
                out[:, place * wide : (place + 1) * wide] = block[...]


def in_order(blocks, me, dim):
    count = len(blocks)
    rows, wide = blocks[0].shape
    shape = (rows * count, wide) if dim == 0 else (rows, wide * count)
    space = pl.ANY if dim == 0 else pltpu.VMEM
    return pl.pallas_call(
        rows_kernel if dim == 0 else columns_kernel,
        out_shape=jax.ShapeDtypeStruct(shape, blocks[0].dtype),
        in_specs=[pl.BlockSpec(memory_space=pltpu.SMEM)]
        + [pl.BlockSpec(memory_space=space)] * count,
        out_specs=pl.BlockSpec(memory_space=pltpu.VMEM),
        scratch_shapes=[pltpu.SemaphoreType.DMA((count,))] if dim == 0 else [],
        compiler_params=pltpu.CompilerParams(vmem_limit_bytes=8 * 1024 * 1024),
        cost_estimate=pl.CostEstimate(
            flops=0, bytes_accessed=4 * rows * wide * count, transcendentals=0
        ),
    )(me[None], *blocks)


def share_kernel(where, *refs):
    blocks, mine, other, sems = refs[:-3], refs[-3], refs[-2], refs[-1]
    count = len(blocks) // 2
    rows = mine.shape[0] // count

    def move(first, second):
        copies = []
        for flip in range(count):
            start = pl.multiple_of((where[1] ^ flip) * rows, 16)
            for layer, out in enumerate((first, second)):
                copies.append(
                    pltpu.make_async_copy(
                        blocks[layer * count + flip].at[pl.ds(0, rows), :],
                        out.at[pl.ds(start, rows), :],
                        sems.at[layer * count + flip],
                    )
                )
        for copy in copies:
            copy.start()
        for copy in copies:
            copy.wait()

    @pl.when(where[0] == 0)
    def _():
        move(mine, other)

    @pl.when(where[0] == 1)
    def _():
        move(other, mine)


def layer_shares(section, group, blocks0, blocks1):
    rows, wide = blocks1[0].shape
    count = len(blocks0)
    out = jax.ShapeDtypeStruct((rows * count, wide), LOW)
    return pl.pallas_call(
        share_kernel,
        out_shape=(out, out),
        in_specs=[pl.BlockSpec(memory_space=pltpu.SMEM)]
        + [pl.BlockSpec(memory_space=pl.ANY)] * (2 * count),
        out_specs=(pl.BlockSpec(memory_space=pltpu.VMEM),) * 2,
        scratch_shapes=[pltpu.SemaphoreType.DMA((2 * count,))],
        compiler_params=pltpu.CompilerParams(vmem_limit_bytes=12 * 1024 * 1024),
        cost_estimate=pl.CostEstimate(
            flops=0, bytes_accessed=8 * rows * wide * count, transcendentals=0
        ),
    )(jnp.stack([section, group]), *blocks0, *blocks1)


def finish_kernel(section, mine, other, down, out, up, qkv, small):
    half = mine.shape[1]

    def fill(low, high):
        for part, columns in ((low, slice(0, half)), (high, slice(half, 2 * half))):
            row = 0
            for result in (down, out, up):
                result[:, columns] = part[row : row + result.shape[0], :].astype(FULL)
                row += result.shape[0]
            for which in range(qkv.shape[0]):
                rows = part[row : row + qkv.shape[2], :].astype(FULL)
                qkv[which, columns, :] = rows.T
                row += qkv.shape[2]
            small[:, columns] = part[row : row + small.shape[0], :].astype(FULL)

    @pl.when(section[0] == 0)
    def _():
        fill(mine, other)

    @pl.when(section[0] == 1)
    def _():
        fill(other, mine)


def finished(section, mine, other, shapes):
    whole = pl.BlockSpec(memory_space=pltpu.VMEM)
    return pl.pallas_call(
        finish_kernel,
        out_shape=[jax.ShapeDtypeStruct(shape, FULL) for shape in shapes],
        in_specs=[pl.BlockSpec(memory_space=pltpu.SMEM), whole, whole],
        out_specs=[whole] * len(shapes),
        compiler_params=pltpu.CompilerParams(vmem_limit_bytes=24 * 1024 * 1024),
        cost_estimate=pl.CostEstimate(
            flops=0, bytes_accessed=12 * mine.size, transcendentals=0
        ),
    )(section[None], mine, other)


def gradient_kernel(section, gelu, mixed, mlp, proj, grad, act, att, small, kept, sent):
    half = kept.shape[1]
    side = section[0]
    for out, place in ((kept, side), (sent, 1 - side)):
        lanes = pl.ds(pl.multiple_of(place * half, half), half)
        row = 0

        def put(left, right):
            out[row : row + left.shape[1], :] = lax.dot_general(
                left, right, (((0,), (0,)), ((), ())), preferred_element_type=FULL
            ).astype(LOW)
            return row + left.shape[1]

        rows_grad = grad[:, lanes]
        row = put(gelu[...], rows_grad)
        row = put(mixed[...], rows_grad)
        row = put(mlp[...], act[:, lanes])
        rows_att = att[:, lanes]
        for which in range(proj.shape[0]):
            row = put(proj[which], rows_att)
        out[row : row + small.shape[0], :] = small[:, lanes].astype(LOW)


def weight_gradients(section, gelu, mixed, mlp, proj, grad, act, att, small):
    width = grad.shape[1]
    rows = gelu.shape[1] + mixed.shape[1] + mlp.shape[1] + proj.shape[0] * proj.shape[2]
    rows += small.shape[0]
    out = jax.ShapeDtypeStruct((rows, width // 2), LOW)
    whole = pl.BlockSpec(memory_space=pltpu.VMEM)
    return pl.pallas_call(
        gradient_kernel,
        out_shape=(out, out),
        in_specs=[pl.BlockSpec(memory_space=pltpu.SMEM)] + [whole] * 8,
        out_specs=(whole, whole),
        compiler_params=pltpu.CompilerParams(vmem_limit_bytes=16 * 1024 * 1024),
        cost_estimate=pl.CostEstimate(
            flops=2 * rows * width * grad.shape[0],
            bytes_accessed=2 * rows * width + 12 * grad.size,
            transcendentals=0,
        ),
    )(section[None], gelu, mixed, mlp, proj, grad, act, att, small)


def rotary_tables(seg_row):
    length = seg_row.shape[-1]
    before = jnp.sum((seg_row[None, :] < seg_row[:, None]).astype(jnp.int32), axis=-1)
    places = jnp.arange(length, dtype=jnp.int32) - before
    halves = ROT // 2
    freqs = jnp.exp(jnp.arange(halves, dtype=FULL) * (-2.0 * math.log(10000.0) / ROT))
    angles = places.astype(FULL)[:, None] * freqs
    return (jnp.cos(angles), jnp.sin(angles))


def rotate(values, cosine, sine):
    halves = cosine.shape[-1]
    first = values[..., :halves]
    second = values[..., halves : 2 * halves]
    cos_rows = cosine[..., None, :]
    sin_rows = sine[..., None, :]
    return jnp.concatenate(
        [
            first * cos_rows - second * sin_rows,
            second * cos_rows + first * sin_rows,
            values[..., 2 * halves :],
        ],
        axis=-1,
    )


def body(
    hidden,
    cotangent,
    segments,
    qkv_weight,
    qkv_bias,
    out_weight,
    out_bias,
    up_weight,
    up_bias,
    down_weight,
    down_bias,
    norm_gain,
    norm_bias,
):
    section = lax.axis_index("pipe")
    member = lax.axis_index("tensor")
    members = lax.axis_size("tensor")
    first_core = section == 0
    length = SEQ_LEN
    local = qkv_weight.shape[3]
    heads = local // HEAD_DIM
    width = qkv_weight.shape[2]
    units = up_weight.shape[2]
    scale = 1.0 / math.sqrt(HEAD_DIM)

    own_rows = lambda rows: lax.dynamic_slice_in_dim(rows, section * length, length, 0)
    state_blocks = received(own_rows(hidden), "tensor")
    target_part, state_blocks[1:] = tie(own_rows(cotangent), state_blocks[1:])
    target_blocks = received(target_part, "tensor")
    state_in = in_order(state_blocks, member, 1)
    seg_row = lax.dynamic_index_in_dim(segments, section, 0, keepdims=False)

    def both(value):
        other = swap(value)
        return (jnp.where(first_core, value, other), jnp.where(first_core, other, value))

    vectors = [qkv_bias, out_bias, up_bias, down_bias, norm_gain, norm_bias]
    packed = both(jnp.concatenate([vector.reshape(-1) for vector in vectors]))
    layers = [[], []]
    for weight in (qkv_weight, out_weight, up_weight, down_weight):
        for layer, value in enumerate(both(weight[0])):
            layers[layer].append(value)
    for layer in range(2):
        start = 0
        for vector in vectors:
            piece = packed[layer][start : start + vector.size].reshape(vector.shape[1:])
            layers[layer].append(piece)
            start += vector.size

    cosine, sine = rotary_tables(seg_row)
    positions = jnp.arange(length, dtype=jnp.int32)
    allowed = (seg_row[:, None] == seg_row[None, :]) & (positions[:, None] >= positions[None, :])

    def masked_scores(queries, key_rows):
        scores = jnp.einsum("qhd,khd->hqk", queries, key_rows, preferred_element_type=FULL)
        return jnp.where(allowed[None], scores * scale, -1e30)

    def forward(state, weights):
        w_qkv, w_out, w_up, w_down, b_qkv, b_out, b_up, b_down, gains, shifts = weights
        center = state - jnp.mean(state, axis=-1, keepdims=True)
        spread = lax.rsqrt(jnp.mean(center * center, axis=-1, keepdims=True) + EPSILON)
        unit = center * spread
        att_low = (unit * gains[0] + shifts[0]).astype(LOW)
        mlp_low = (unit * gains[1] + shifts[1]).astype(LOW)
        projected = (
            jnp.einsum("td,cde->cte", att_low, w_qkv, preferred_element_type=FULL)
            + b_qkv[:, None, :]
        ).reshape(3, length, heads, HEAD_DIM)
        queries = rotate(projected[0], cosine, sine).astype(LOW)
        key_rows = rotate(projected[1], cosine, sine).astype(LOW)
        value_rows = projected[2].astype(LOW)
        masked = masked_scores(queries, key_rows)
        peak = jnp.max(masked, axis=-1, keepdims=True)
        exponent = jnp.exp(masked - peak)
        totals = jnp.sum(exponent, axis=-1, keepdims=True)
        log_total = peak + jnp.log(totals)
        probs_low = (exponent / totals).astype(LOW)
        mixed = jnp.einsum("hqk,khd->qhd", probs_low, value_rows, preferred_element_type=FULL)
        mixed = mixed.reshape(length, local).astype(LOW)
        activation = jnp.dot(mlp_low, w_up, preferred_element_type=FULL) + b_up
        gelu_low = jax.nn.gelu(activation, approximate=False).astype(LOW)
        branch = jnp.dot(mixed, w_out, preferred_element_type=FULL) + jnp.dot(
            gelu_low, w_down, preferred_element_type=FULL
        )
        saved = (
            unit,
            spread,
            att_low,
            mlp_low,
            queries,
            key_rows,
            value_rows,
            log_total,
            mixed,
            activation,
            gelu_low,
        )
        return branch.astype(LOW), saved

    def backward(grad_low, weights, saved):
        w_qkv, w_out, w_up, w_down, b_qkv, b_out, b_up, b_down, gains, shifts = weights
        (
            unit,
            spread,
            att_low,
            mlp_low,
            queries,
            key_rows,
            value_rows,
            log_total,
            mixed,
            activation,
            gelu_low,
        ) = saved
        d_gelu = jnp.einsum("td,fd->tf", grad_low, w_down, preferred_element_type=FULL)
        gelu_slope = 0.5 * (1.0 + lax.erf(activation * math.sqrt(0.5))) + activation * (
            jnp.exp(-0.5 * activation * activation) * (1.0 / math.sqrt(2.0 * math.pi))
        )
        d_act = (d_gelu * gelu_slope).astype(LOW)
        d_mixed = jnp.einsum("td,ed->te", grad_low, w_out, preferred_element_type=FULL)
        d_mixed = d_mixed.astype(LOW).reshape(length, heads, HEAD_DIM)
        probs = jnp.exp(masked_scores(queries, key_rows) - log_total)
        d_probs = jnp.einsum("qhd,khd->hqk", d_mixed, value_rows, preferred_element_type=FULL)
        middle = jnp.sum(d_probs * probs, axis=-1, keepdims=True)
        d_scores = (probs * (d_probs - middle)).astype(LOW)
        d_queries = jnp.einsum("hqk,khd->qhd", d_scores, key_rows, preferred_element_type=FULL)
        d_keys = jnp.einsum("hqk,qhd->khd", d_scores, queries, preferred_element_type=FULL)
        d_values = jnp.einsum(
            "hqk,qhd->khd", probs.astype(LOW), d_mixed, preferred_element_type=FULL
        )
        d_proj = (
            jnp.stack(
                [
                    rotate(d_queries * scale, cosine, -sine),
                    rotate(d_keys * scale, cosine, -sine),
                    d_values,
                ]
            )
            .astype(LOW)
            .reshape(3, length, local)
        )
        d_att = jnp.einsum("cte,cde->td", d_proj, w_qkv, preferred_element_type=FULL)
        d_mlp = jnp.einsum("tf,df->td", d_act, w_up, preferred_element_type=FULL)
        d_unit = d_att * gains[0] + d_mlp * gains[1]
        norm_rows = jnp.stack(
            [
                jnp.sum(d_att * unit, axis=0),
                jnp.sum(d_mlp * unit, axis=0),
                jnp.sum(d_att, axis=0),
                jnp.sum(d_mlp, axis=0),
            ]
        )
        small = jnp.stack(
            [
                jnp.sum(grad_low.astype(FULL), axis=0),
                jnp.sum(d_act.astype(FULL), axis=0),
                jnp.pad(
                    jnp.sum(d_proj.astype(FULL), axis=1).reshape(-1), (0, width - 3 * local)
                ),
            ]
        )
        small = jnp.pad(small, ((0, 64 - small.shape[0]), (0, 0)))
        return d_unit, norm_rows, (gelu_low, mixed, mlp_low, d_proj, grad_low, d_act, att_low, small)

    def group_shares(kept, arrived, group):
        groups = lax.axis_size("dp")
        if groups > 4:
            total = (kept.astype(FULL) + arrived.astype(FULL)).astype(LOW)
            return [lax.psum_scatter(total, "dp", scatter_dimension=0, tiled=True)]
        rows = kept.shape[0] // groups

        def piece_of(place):
            terms = [
                lax.dynamic_slice_in_dim(part, place * rows, rows, 0).astype(FULL)
                for part in (kept, arrived)
            ]
            return (terms[0] + terms[1]).astype(LOW)

        return scattered(piece_of, "dp", group)

    def all_shares(share):
        if lax.axis_size("dp") > 4:
            return [lax.all_gather(share, "dp", axis=0, tiled=True)]
        return received(share, "dp")

    rows_part = length // members
    token_parts = lambda values: scattered(
        lambda place: lax.dynamic_slice_in_dim(values, place * rows_part, rows_part, 0),
        "tensor",
        member,
    )
    feature_parts = lambda values, me: scattered(
        lambda place: lax.dynamic_slice_in_dim(values, place * local, local, 1), "tensor", me
    )
    own_features = lambda values: lax.dynamic_slice_in_dim(values, member * local, local, 1)
    own_tokens = lambda values: lax.dynamic_slice_in_dim(values, member * rows_part, rows_part, 0)

    first, second = layers
    branch0, saved0 = forward(state_in.astype(FULL), first)
    branch0, target_blocks = tie(branch0, target_blocks)
    terms0 = token_parts(branch0)
    target = in_order(target_blocks, member, 1)
    out0 = own_tokens(state_in).astype(FULL) + total_of(terms0) + first[5] + first[7]
    state1 = lax.all_gather(out0.astype(LOW), "tensor", axis=0, tiled=True)
    branch1, saved1 = forward(state1.astype(FULL), second)

    def moments(d_unit, unit):
        return jnp.stack([jnp.mean(d_unit, axis=-1), jnp.mean(d_unit * unit, axis=-1)], axis=-1)

    d_unit1, norm1, inputs1 = backward(target, second, saved1)
    terms1 = token_parts(d_unit1.astype(LOW))
    kept1, sent1 = weight_gradients(section, *inputs1)
    arrived1 = swap(sent1)
    d_sum1 = total_of(terms1)
    unit1 = own_tokens(saved1[0])
    part1 = moments(d_sum1, unit1)
    d_in1 = own_tokens(target).astype(FULL) + own_tokens(saved1[1]) * (
        d_sum1 - part1[:, :1] - unit1 * part1[:, 1:]
    )
    group = lax.axis_index("dp")
    share1 = total_of(group_shares(kept1, arrived1, group)).astype(LOW)
    grad0 = lax.all_gather(d_in1.astype(LOW), "tensor", axis=0, tiled=True)
    grad0, share1, branch1 = tie(grad0, share1, branch1)
    terms_out = feature_parts(branch1, member)

    d_unit0, norm0, inputs0 = backward(grad0, first, saved0)
    all1 = all_shares(share1)
    kept0, sent0 = weight_gradients(section, *inputs0)
    all1, terms_out, sent0 = tie(all1, terms_out, sent0)
    out1 = (
        own_features(state1).astype(FULL)
        + total_of(terms_out)
        + own_features((second[5] + second[7])[None])
    )
    arrived0 = swap(sent0)
    shares0 = group_shares(kept0, arrived0, group)

    member0, arrived0 = tie(member, arrived0)
    d_low0 = d_unit0.astype(LOW)
    norm_columns = jnp.concatenate([norm0, norm1]).reshape(length, -1)
    part0 = jnp.concatenate([moments(d_low0.astype(FULL), saved0[0]), norm_columns], axis=1)
    part0 = part0.astype(LOW)
    terms0 = scattered(
        lambda place: jnp.concatenate(
            [lax.dynamic_slice_in_dim(d_low0, place * local, local, 1), part0], axis=1
        ),
        "tensor",
        member0,
    )
    shares0, terms0 = tie(shares0, terms0)
    d_sum0 = total_of(terms0)
    rows0 = jnp.concatenate(
        [total_of(shares0), d_sum0[:, local + 2 :].reshape(16, width // 2)]
    ).astype(LOW)
    groups = lax.axis_size("dp")
    if groups > 4:
        all0 = all_shares(rows0[:-16])
        norm_sum = lax.psum(rows0[-16:].astype(FULL), "dp")
    else:
        all0 = all_shares(rows0)
        norm_sum = pair_sum([block[-16:].astype(FULL) for block in all0])
    norm_sum = (norm_sum + swap(norm_sum)).reshape(8, width)
    norm_rows = jnp.where(first_core, norm_sum[:4], norm_sum[4:])
    part0 = d_sum0[:, local:]
    d_in0 = own_features(grad0).astype(FULL) + saved0[1] * (
        d_sum0[:, :local] - part0[:, :1] - own_features(saved0[0]) * part0[:, 1:2]
    )

    mine, other = layer_shares(section, group, all0, all1)
    g_down, g_out, g_up, g_qkv, small = finished(
        section,
        mine,
        swap(other),
        [
            down_weight.shape[1:],
            out_weight.shape[1:],
            up_weight.shape[1:],
            qkv_weight.shape[1:],
            (64, width),
        ],
    )
    own0, own1 = own_features(state1), out1.astype(LOW)
    d_own1 = own_features(grad0)
    rows_sent = jnp.where(
        first_core,
        jnp.concatenate([own1, d_own1], axis=1),
        jnp.concatenate([own0, d_in0.astype(LOW)], axis=1),
    )
    rows_other = swap(rows_sent)
    state_other, d_other = rows_other[:, :local], rows_other[:, local:].astype(FULL)

    def both_parts(low_value, high_value, arrived):
        mine = jnp.where(first_core, low_value, high_value)
        return jnp.concatenate(
            [jnp.where(first_core, mine, arrived), jnp.where(first_core, arrived, mine)]
        )[None]

    states_out = both_parts(own0, own1, state_other)
    d_states_out = both_parts(d_in0, d_own1.astype(FULL), d_other)
    return (
        states_out,
        d_states_out,
        g_qkv[None],
        small[2, : 3 * local].reshape(qkv_bias.shape),
        g_out[None],
        small[0][None],
        g_up[None],
        small[1][None],
        g_down[None],
        small[0][None],
        norm_rows[0:2][None],
        norm_rows[2:4][None],
    )


def solution(mesh):
    in_specs = (
        P("dp", "tensor"),
        P("dp", "tensor"),
        P("dp", None),
        P("pipe", None, None, "tensor"),
        P("pipe", None, "tensor"),
        P("pipe", "tensor", None),
        P("pipe", None),
        P("pipe", None, "tensor"),
        P("pipe", "tensor"),
        P("pipe", "tensor", None),
        P("pipe", None),
        P("pipe", None, None),
        P("pipe", None, None),
    )
    out_specs = (
        P("pipe", "dp", "tensor"),
        P("pipe", "dp", "tensor"),
        P("pipe", None, None, "tensor"),
        P("pipe", None, "tensor"),
        P("pipe", "tensor", None),
        P("pipe", None),
        P("pipe", None, "tensor"),
        P("pipe", "tensor"),
        P("pipe", "tensor", None),
        P("pipe", None),
        P("pipe", None, None),
        P("pipe", None, None),
    )
    return jax.shard_map(body, mesh=mesh, in_specs=in_specs, out_specs=out_specs, check_vma=False)
```

```python
from functools import partial
import math

import jax
import jax.numpy as jnp
import numpy as np
from jax import lax
from jax.experimental import pallas as pl
from jax.experimental.pallas import tpu as pltpu
from jax.sharding import PartitionSpec as P

HEAD_DIM = 64
ROT = 16
SEQ_LEN = 512
EPSILON = 1e-05
SMALL_ROWS = 64
LOW = jnp.bfloat16
FULL = jnp.float32


def swap(value):
    return lax.ppermute(value, "pipe", [(0, 1), (1, 0)])


def partner(value, axis, flip):
    count = lax.axis_size(axis)
    return lax.ppermute(value, axis, [(source, source ^ flip) for source in range(count)])


def pair_sum(terms):
    while len(terms) > 1:
        terms = [first + second for first, second in zip(terms[0::2], terms[1::2])]
    return terms[0]


def scattered(piece_of, axis, me):
    terms = [piece_of(me)]
    for flip in range(1, lax.axis_size(axis)):
        terms.append(partner(piece_of(me ^ flip), axis, flip))
    return terms


def total_of(terms):
    return pair_sum([term.astype(FULL) for term in terms])


def received(value, axis):
    return [value] + [partner(value, axis, flip) for flip in range(1, lax.axis_size(axis))]


def tie(*values):
    return lax.optimization_barrier(values)


def rows_kernel(me, *refs):
    blocks, out, sems = refs[:-2], refs[-2], refs[-1]
    rows = blocks[0].shape[0]
    copies = []
    for flip, block in enumerate(blocks):
        start = pl.multiple_of((me[0] ^ flip) * rows, 16)
        copies.append(
            pltpu.make_async_copy(block, out.at[pl.ds(start, rows), :], sems.at[flip])
        )
    for copy in copies:
        copy.start()
    for copy in copies:
        copy.wait()


def columns_kernel(me, *refs):
    blocks, out = refs[:-1], refs[-1]
    wide = blocks[0].shape[0]
    for place in range(len(blocks)):
        for flip, block in enumerate(blocks):

            @pl.when(me[0] == place ^ flip)
            def _():
                out[:, place * wide : (place + 1) * wide] = block[...].T


def in_order(blocks, me, dim):
    count = len(blocks)
    rows, wide = blocks[0].shape
    shape = (rows * count, wide) if dim == 0 else (wide, rows * count)
    space = pl.ANY if dim == 0 else pltpu.VMEM
    return pl.pallas_call(
        rows_kernel if dim == 0 else columns_kernel,
        out_shape=jax.ShapeDtypeStruct(shape, blocks[0].dtype),
        in_specs=[pl.BlockSpec(memory_space=pltpu.SMEM)]
        + [pl.BlockSpec(memory_space=space)] * count,
        out_specs=pl.BlockSpec(memory_space=pltpu.VMEM),
        scratch_shapes=[pltpu.SemaphoreType.DMA((count,))] if dim == 0 else [],
        compiler_params=pltpu.CompilerParams(vmem_limit_bytes=8 * 1024 * 1024),
        cost_estimate=pl.CostEstimate(
            flops=0, bytes_accessed=4 * rows * wide * count, transcendentals=0
        ),
    )(me[None], *blocks)


def finish_kernel(where, *refs):
    count = (len(refs) - 14) // 3
    first, second, arrived = refs[:count], refs[count : 2 * count], refs[2 * count : 3 * count]
    outs, results = refs[3 * count : 3 * count + 5], refs[3 * count + 5 : 3 * count + 10]
    mine, other, sems, out_sems = refs[3 * count + 10 :]
    down, out, up, qkv, small = results
    rows = mine.shape[0] // count
    half = mine.shape[1]

    def place(index):
        start = (where[1] ^ index) * rows if count > 1 else 0
        return pl.ds(pl.multiple_of(start, 16), rows)

    for layer, blocks in enumerate((first, second)):

        @pl.when(where[0] == layer)
        def _():
            for index, block in enumerate(blocks):
                pltpu.make_async_copy(
                    block.at[pl.ds(0, rows), :], mine.at[place(index), :], sems.at[index]
                ).start()

    loads = [
        pltpu.make_async_copy(block, other.at[place(index), :], sems.at[count + index])
        for index, block in enumerate(arrived)
    ]
    for load in loads:
        load.start()
    for index, block in enumerate(second):
        pltpu.make_async_copy(
            block.at[pl.ds(0, rows), :], mine.at[place(index), :], sems.at[index]
        ).wait()
    for load in loads:
        load.wait()

    own_start = pl.multiple_of(where[0] * half, half)
    other_start = pl.multiple_of((1 - where[0]) * half, half)
    parts = ((mine, pl.ds(own_start, half)), (other, pl.ds(other_start, half)))
    row = 0
    for index, result in enumerate((down, out, up)):
        for part, columns in parts:
            result[:, columns] = part[row : row + result.shape[0], :].astype(FULL)
        row += result.shape[0]
        pltpu.make_async_copy(result, outs[index], out_sems.at[index]).start()
    for which in range(qkv.shape[0]):
        for part, columns in parts:
            qkv[which, :, columns] = part[row : row + qkv.shape[1], :].astype(FULL)
        row += qkv.shape[1]
    pltpu.make_async_copy(qkv, outs[3], out_sems.at[3]).start()
    for part, columns in parts:
        small[:, columns] = part[row : row + small.shape[0], :].astype(FULL)
    pltpu.make_async_copy(small, outs[4], out_sems.at[4]).start()
    for index, result in enumerate(results):
        pltpu.make_async_copy(result, outs[index], out_sems.at[index]).wait()


def finished(section, group, first, second, arrived, shapes):
    hbm = pl.BlockSpec(memory_space=pltpu.HBM)
    count = len(first)
    rows, half = arrived[0].shape
    return pl.pallas_call(
        finish_kernel,
        out_shape=[jax.ShapeDtypeStruct(shape, FULL) for shape in shapes],
        in_specs=[pl.BlockSpec(memory_space=pltpu.SMEM)]
        + [pl.BlockSpec(memory_space=pl.ANY)] * (3 * count),
        out_specs=[hbm] * len(shapes),
        scratch_shapes=[pltpu.VMEM(shape, FULL) for shape in shapes]
        + [pltpu.VMEM((rows * count, half), LOW)] * 2
        + [pltpu.SemaphoreType.DMA((2 * count,)), pltpu.SemaphoreType.DMA((len(shapes),))],
        compiler_params=pltpu.CompilerParams(vmem_limit_bytes=60 * 1024 * 1024),
        cost_estimate=pl.CostEstimate(
            flops=0, bytes_accessed=12 * rows * half * count, transcendentals=0
        ),
    )(jnp.stack([section, group]), *first, *second, *arrived)


def rotary_tables(seg_row, heads):
    length = seg_row.shape[-1]
    before = jnp.sum((seg_row[None, :] < seg_row[:, None]).astype(jnp.int32), axis=-1)
    places = jnp.arange(length, dtype=jnp.int32) - before
    halves = ROT // 2
    freqs = jnp.exp(jnp.arange(halves, dtype=FULL) * (-2.0 * math.log(10000.0) / ROT))
    angles = places.astype(FULL)[:, None] * freqs
    rest = HEAD_DIM - ROT
    cosine = jnp.concatenate([jnp.cos(angles)] * 2 + [jnp.ones((length, rest), FULL)], axis=1)
    sine = jnp.concatenate([jnp.sin(angles)] * 2 + [jnp.zeros((length, rest), FULL)], axis=1)
    return jnp.tile(cosine, (1, heads)), jnp.tile(sine, (1, heads))


def partner_matrix(heads):
    matrix = np.zeros((heads * HEAD_DIM, heads * HEAD_DIM), np.float32)
    for head in range(heads):
        for lane in range(ROT // 2):
            first = head * HEAD_DIM + lane
            second = first + ROT // 2
            matrix[second, first] = -1.0
            matrix[first, second] = 1.0
    return jnp.asarray(matrix, LOW)


def product(left, right, left_dim=1, right_dim=0):
    return lax.dot_general(
        left, right, (((left_dim,), (right_dim,)), ((), ())), preferred_element_type=FULL
    )


def fetch(section, layer, owns, others, places, sems):
    @pl.when(section[0] == layer)
    def _():
        for index, (own, place) in enumerate(zip(owns, places)):
            pltpu.make_async_copy(own, place, sems.at[index]).start()

    @pl.when(section[0] != layer)
    def _():
        for index, (other, place) in enumerate(zip(others, places)):
            pltpu.make_async_copy(other, place, sems.at[index]).start()


def arrive(owns, places, sems, index):
    pltpu.make_async_copy(owns[index], places[index], sems.at[index]).wait()


def head_lanes(values, head):
    lanes = lax.broadcasted_iota(jnp.int32, values.shape, 1)
    return (lanes >= head * HEAD_DIM) & (lanes < (head + 1) * HEAD_DIM)


def masked_scores(queries, key_rows, seg_column, seg_line, start):
    scores = product(queries, key_rows, 1, 1) * (1.0 / math.sqrt(HEAD_DIM))
    rows = start + lax.broadcasted_iota(jnp.int32, scores.shape, 0)
    columns = lax.broadcasted_iota(jnp.int32, scores.shape, 1)
    return jnp.where((seg_column == seg_line) & (rows >= columns), scores, -1e30)


STEP = 32
BLOCK = 256


def forward_kernel(layer, section, vecs, bias, matrix, line, *refs):
    state_in, cosine_in, sine_in, column_in = refs[0:4]
    owns, others, outs = refs[4:8], refs[8:12], refs[12:18]
    places, sems, out_sems = refs[18:22], refs[22], refs[23]
    state, cosine, sine, column = refs[24:28]
    results = refs[28:34]
    branch, qkv, stats, mixed, gelu, slope = results
    att, mlp, wide = refs[34:37]
    w_qkv, w_out, w_up, w_down = places
    length = state.shape[0]
    loads = [
        pltpu.make_async_copy(source, place, sems.at[4 + index])
        for index, (source, place) in enumerate(
            zip((state_in, cosine_in, sine_in, column_in), (state, cosine, sine, column))
        )
    ]
    loads[0].start()
    fetch(section, layer, owns, others, places, sems)
    for load in loads[1:]:
        load.start()
    stores = [
        pltpu.make_async_copy(result, out, out_sems.at[index])
        for index, (result, out) in enumerate(zip(results, outs))
    ]
    loads[0].wait()

    def normed(step, carry):
        rows = pl.ds(pl.multiple_of(step * STEP, STEP), STEP)
        values = state[rows, :].astype(FULL)
        mean = jnp.mean(values, axis=-1, keepdims=True)
        center = values - mean
        spread = lax.rsqrt(jnp.mean(center * center, axis=-1, keepdims=True) + EPSILON)
        unit = center * spread
        att[rows, :] = (unit * vecs[0:1, :] + vecs[2:3, :]).astype(LOW)
        mlp[rows, :] = (unit * vecs[1:2, :] + vecs[3:4, :]).astype(LOW)
        stats[rows, 3:4] = mean
        stats[rows, 4:5] = spread
        return carry

    lax.fori_loop(0, length // STEP, normed, 0)

    loads[1].wait()
    loads[2].wait()
    arrive(owns, places, sems, 0)
    for which in range(3):
        values = product(att[...], w_qkv[which], 1, 1) + bias[which : which + 1, :]
        if which < 2:
            high = values.astype(LOW)
            small = (values - high.astype(FULL)).astype(LOW)
            turned = product(high, matrix[...]) + product(small, matrix[...])
            values = values * cosine[...] + turned * sine[...]
        qkv[which] = values.astype(LOW)
    stores[1].start()
    loads[3].wait()

    for start in range(0, length, BLOCK):
        rows, keys = slice(start, start + BLOCK), slice(0, start + BLOCK)
        queries = qkv[0, rows, :]
        found = jnp.zeros(queries.shape, FULL)
        for head in range(queries.shape[1] // HEAD_DIM):
            own = head_lanes(queries, head)
            scores = masked_scores(
                jnp.where(own, queries, jnp.zeros_like(queries)),
                qkv[1, keys, :],
                column[rows, :],
                line[:, keys],
                start,
            )
            peak = jnp.max(scores, axis=-1, keepdims=True)
            exponent = jnp.exp(scores - peak)
            totals = jnp.sum(exponent, axis=-1, keepdims=True)
            stats[rows, head : head + 1] = peak + jnp.log(totals)
            probs = (exponent / totals).astype(LOW)
            found = jnp.where(own, product(probs, qkv[2, keys, :]), found)
        mixed[rows, :] = found.astype(LOW)
    stores[2].start()
    stores[3].start()

    arrive(owns, places, sems, 2)
    wide[...] = product(mlp[...], w_up[...])

    def activated(step, carry):
        rows = pl.ds(pl.multiple_of(step * STEP, STEP), STEP)
        values = wide[rows, :] + vecs[4:5, :]
        share = 0.5 + 0.5 * lax.erf(values * math.sqrt(0.5))
        bell = jnp.exp(-0.5 * values * values) * (1.0 / math.sqrt(2.0 * math.pi))
        gelu[rows, :] = (values * share).astype(LOW)
        slope[rows, :] = (share + values * bell).astype(LOW)
        return carry

    lax.fori_loop(0, length // STEP, activated, 0)
    stores[4].start()
    stores[5].start()

    arrive(owns, places, sems, 1)
    arrive(owns, places, sems, 3)
    branch[...] = (product(mixed[...], w_out[...]) + product(gelu[...], w_down[...])).astype(LOW)
    stores[0].start()
    for store in stores:
        store.wait()


def backward_kernel(layer, section, vecs, matrix, line, *refs):
    sources, owns, others = refs[0:10], refs[10:14], refs[14:18]
    moments, norms, outs = refs[18], refs[19], refs[20:23]
    places, sems, out_sems = refs[23:27], refs[27], refs[28]
    held = refs[29:39]
    stats, state, grad, slope, qkv, column, cosine, sine, mixed, gelu = held
    results = refs[39:42]
    d_low, sent, kept = results
    att, mlp, unit, d_act, proj, small = refs[42:48]
    wide, second, d_queries, d_keys, d_values, d_mixed = refs[48:54]
    w_qkv, w_out, w_up, w_down = places
    length, width = state.shape
    loads = [
        pltpu.make_async_copy(source, place, sems.at[4 + index])
        for index, (source, place) in enumerate(zip(sources, held))
    ]
    for load in loads[:3]:
        load.start()
    fetch(section, layer, owns, others, places, sems)
    for load in loads[3:]:
        load.start()
    stores = [
        pltpu.make_async_copy(result, out, out_sems.at[index])
        for index, (result, out) in enumerate(zip(results, outs))
    ]
    loads[0].wait()
    loads[1].wait()

    def normed(step, carry):
        rows = pl.ds(pl.multiple_of(step * STEP, STEP), STEP)
        values = (state[rows, :].astype(FULL) - stats[rows, 3:4]) * stats[rows, 4:5]
        unit[rows, :] = values
        att[rows, :] = (values * vecs[0:1, :] + vecs[2:3, :]).astype(LOW)
        mlp[rows, :] = (values * vecs[1:2, :] + vecs[3:4, :]).astype(LOW)
        return carry

    lax.fori_loop(0, length // STEP, normed, 0)
    fold = lambda values: jnp.sum(values.reshape(STEP // 8, 8, values.shape[1]), axis=0)

    loads[2].wait()
    arrive(owns, places, sems, 1)
    d_mixed[...] = product(grad[...], w_out[...], 1, 1).astype(LOW)
    arrive(owns, places, sems, 3)
    wide[...] = product(grad[...], w_down[...], 1, 1)
    loads[3].wait()

    def activated(step, carry):
        rows = pl.ds(pl.multiple_of(step * STEP, STEP), STEP)
        values = (wide[rows, :] * slope[rows, :].astype(FULL)).astype(LOW)
        d_act[rows, :] = values
        return carry[0] + fold(values.astype(FULL)), carry[1] + fold(grad[rows, :].astype(FULL))

    zero = jnp.zeros((8, width), FULL)
    act_sum, grad_sum = lax.fori_loop(0, length // STEP, activated, (zero, zero))

    loads[4].wait()
    loads[5].wait()
    d_keys[...] = jnp.zeros_like(d_keys)
    d_values[...] = jnp.zeros_like(d_values)
    for start in range(0, length, BLOCK):
        rows, keys = slice(start, start + BLOCK), slice(0, start + BLOCK)
        queries, upper = qkv[0, rows, :], d_mixed[rows, :]
        key_rows, value_rows = qkv[1, keys, :], qkv[2, keys, :]
        found = jnp.zeros(queries.shape, FULL)
        for head in range(queries.shape[1] // HEAD_DIM):
            own = head_lanes(queries, head)
            clear = jnp.zeros_like(queries)
            own_queries, own_upper = jnp.where(own, queries, clear), jnp.where(own, upper, clear)
            scores = masked_scores(own_queries, key_rows, column[rows, :], line[:, keys], start)
            probs = jnp.exp(scores - stats[rows, head : head + 1])
            d_probs = product(own_upper, value_rows, 1, 1)
            middle = jnp.sum(d_probs * probs, axis=-1, keepdims=True)
            d_scores = (probs * (d_probs - middle)).astype(LOW)
            found = jnp.where(own, product(d_scores, key_rows), found)
            d_keys[keys, :] += product(d_scores, own_queries, 0, 0)
            d_values[keys, :] += product(probs.astype(LOW), own_upper, 0, 0)
        d_queries[rows, :] = found

    loads[6].wait()
    loads[7].wait()
    scale = 1.0 / math.sqrt(HEAD_DIM)
    for which, source in enumerate((d_queries, d_keys)):
        values = (source[...] * scale).astype(LOW)
        turned = product(values, matrix[...])
        proj[which] = (values.astype(FULL) * cosine[...] - turned * sine[...]).astype(LOW)
    proj[2] = d_values[...].astype(LOW)

    arrive(owns, places, sems, 2)
    second[...] = product(d_act[...], w_up[...], 1, 1)
    arrive(owns, places, sems, 0)
    wide[...] = (
        product(proj[0], w_qkv[0]) + product(proj[1], w_qkv[1]) + product(proj[2], w_qkv[2])
    )

    def joined(step, carry):
        rows = pl.ds(pl.multiple_of(step * STEP, STEP), STEP)
        d_att, d_mlp, values = wide[rows, :], second[rows, :], unit[rows, :]
        total = (d_att * vecs[0:1, :] + d_mlp * vecs[1:2, :]).astype(LOW)
        d_low[rows, :] = total
        total = total.astype(FULL)
        moments[rows, 0:1] = jnp.mean(total, axis=-1, keepdims=True)
        moments[rows, 1:2] = jnp.mean(total * values, axis=-1, keepdims=True)
        return (
            carry[0] + fold(d_att * values),
            carry[1] + fold(d_mlp * values),
            carry[2] + fold(d_att),
            carry[3] + fold(d_mlp),
        )

    sums = lax.fori_loop(0, length // STEP, joined, (zero,) * 4)
    stores[0].start()
    for index, rows in enumerate(sums):
        norms[index : index + 1, :] = jnp.sum(rows, axis=0, keepdims=True)

    small[...] = jnp.zeros_like(small)
    small[0:1, :] = jnp.sum(grad_sum, axis=0, keepdims=True)
    small[1:2, :] = jnp.sum(act_sum, axis=0, keepdims=True)
    for which in range(3):
        small[2 + which : 3 + which, 0 : proj.shape[2]] = jnp.sum(
            proj[which].astype(FULL), axis=0, keepdims=True
        )

    loads[8].wait()
    loads[9].wait()
    half = kept.shape[1]
    side = section[0]
    for out, place, store in ((sent, 1 - side, stores[1]), (kept, side, stores[2])):
        lanes = pl.ds(pl.multiple_of(place * half, half), half)
        row = 0

        def put(left, right):
            out[row : row + left.shape[1], :] = product(left, right, 0, 0).astype(LOW)
            return row + left.shape[1]

        rows_grad = grad[:, lanes]
        row = put(gelu[...], rows_grad)
        row = put(mixed[...], rows_grad)
        row = put(mlp[...], d_act[:, lanes])
        rows_att = att[:, lanes]
        for which in range(proj.shape[0]):
            row = put(proj[which], rows_att)
        out[row : row + small.shape[0], :] = small[:, lanes].astype(LOW)
        store.start()
    for store in stores:
        store.wait()


def on_core(count):
    return [pl.BlockSpec(memory_space=pltpu.VMEM)] * count


def in_memory(count):
    return [pl.BlockSpec(memory_space=pltpu.HBM)] * count


def buffers(arrays):
    return [pltpu.VMEM(array.shape, array.dtype) for array in arrays]


def forward(layer, section, state, vecs, bias, tables, owns, others):
    cosine, sine, matrix, column, line = tables
    length, width = state.shape
    local, units = owns[0].shape[1], owns[2].shape[1]
    shape = jax.ShapeDtypeStruct
    outs = [
        shape((length, width), LOW),
        shape((3, length, local), LOW),
        shape((length, 128), FULL),
        shape((length, local), LOW),
        shape((length, units), LOW),
        shape((length, units), LOW),
    ]
    sources = [state, cosine, sine, column]
    return pl.pallas_call(
        partial(forward_kernel, layer),
        out_shape=outs,
        in_specs=[pl.BlockSpec(memory_space=pltpu.SMEM)]
        + on_core(4)
        + [pl.BlockSpec(memory_space=pl.ANY)]
        + in_memory(11),
        out_specs=in_memory(len(outs)),
        scratch_shapes=buffers(owns)
        + [pltpu.SemaphoreType.DMA((8,)), pltpu.SemaphoreType.DMA((len(outs),))]
        + buffers(sources)
        + buffers(outs)
        + [
            pltpu.VMEM((length, width), LOW),
            pltpu.VMEM((length, width), LOW),
            pltpu.VMEM((length, units), FULL),
        ],
        compiler_params=pltpu.CompilerParams(vmem_limit_bytes=60 * 1024 * 1024),
        cost_estimate=pl.CostEstimate(
            flops=2 * length * sum(own.size for own in owns),
            bytes_accessed=2 * sum(own.size for own in owns) + 12 * length * width,
            transcendentals=2 * length * units,
        ),
    )(section[None], vecs, bias, matrix, line, *sources, *owns, *others)


def backward(layer, section, grad, state, vecs, tables, saved, owns, others):
    cosine, sine, matrix, column, line = tables
    qkv, stats, mixed, gelu, slope = saved
    length, width = state.shape
    local, units = owns[0].shape[1], owns[2].shape[1]
    shape = jax.ShapeDtypeStruct
    rows = units + local + width + 3 * local + SMALL_ROWS
    outs = [
        shape((length, 2), FULL),
        shape((4, width), FULL),
        shape((length, width), LOW),
        shape((rows, width // 2), LOW),
        shape((rows, width // 2), LOW),
    ]
    sources = [stats, state, grad, slope, qkv, column, cosine, sine, mixed, gelu]
    anywhere = [pl.BlockSpec(memory_space=pl.ANY)]
    return pl.pallas_call(
        partial(backward_kernel, layer),
        out_shape=outs,
        in_specs=[pl.BlockSpec(memory_space=pltpu.SMEM)]
        + on_core(3)
        + in_memory(1)
        + anywhere * 2
        + in_memory(15),
        out_specs=on_core(2) + in_memory(3),
        scratch_shapes=buffers(owns)
        + [pltpu.SemaphoreType.DMA((14,)), pltpu.SemaphoreType.DMA((3,))]
        + buffers(sources)
        + buffers(outs[2:])
        + [
            pltpu.VMEM((length, width), LOW),
            pltpu.VMEM((length, width), LOW),
            pltpu.VMEM((length, width), FULL),
            pltpu.VMEM((length, units), LOW),
            pltpu.VMEM((3, length, local), LOW),
            pltpu.VMEM((SMALL_ROWS, width), FULL),
            pltpu.VMEM((length, units), FULL),
            pltpu.VMEM((length, width), FULL),
            pltpu.VMEM((length, local), FULL),
            pltpu.VMEM((length, local), FULL),
            pltpu.VMEM((length, local), FULL),
            pltpu.VMEM((length, local), LOW),
        ],
        compiler_params=pltpu.CompilerParams(vmem_limit_bytes=60 * 1024 * 1024),
        cost_estimate=pl.CostEstimate(
            flops=4 * length * sum(own.size for own in owns),
            bytes_accessed=4 * sum(own.size for own in owns) + 12 * length * width,
            transcendentals=2 * length * units,
        ),
    )(section[None], vecs, matrix, line, *sources, *owns, *others)


def body(
    hidden,
    cotangent,
    segments,
    qkv_weight,
    qkv_bias,
    out_weight,
    out_bias,
    up_weight,
    up_bias,
    down_weight,
    down_bias,
    norm_gain,
    norm_bias,
):
    section = lax.axis_index("pipe")
    member = lax.axis_index("tensor")
    members = lax.axis_size("tensor")
    first_core = section == 0
    length = SEQ_LEN
    local = qkv_weight.shape[3]
    heads = local // HEAD_DIM
    width = qkv_weight.shape[2]
    units = up_weight.shape[2]
    scale = 1.0 / math.sqrt(HEAD_DIM)

    own_rows = lambda rows: lax.dynamic_slice_in_dim(rows, section * length, length, 0)
    state_in = lax.all_gather(own_rows(hidden), "tensor", axis=1, tiled=True)
    target_part, state_in = tie(own_rows(cotangent), state_in)
    target_blocks = received(target_part.T, "tensor")
    seg_row = lax.dynamic_index_in_dim(segments, section, 0, keepdims=False)

    owns = [weight[0] for weight in (qkv_weight, out_weight, up_weight, down_weight)]
    owns[0] = owns[0].swapaxes(1, 2)
    others = [swap(own) for own in owns]
    one_row = lambda vector: jnp.pad(vector, ((0, 0), (0, width - vector.shape[1])))
    vecs = jnp.concatenate(
        [
            norm_gain[0],
            norm_bias[0],
            up_bias,
            out_bias + down_bias,
            one_row(qkv_bias.reshape(1, -1)),
            jnp.zeros((1, width), FULL),
        ]
    )
    other_vecs = swap(vecs)
    vecs = [
        jnp.where(first_core, vecs, other_vecs),
        jnp.where(first_core, other_vecs, vecs),
    ]
    biases = [rows[6, : 3 * local].reshape(3, local) for rows in vecs]
    tables = (
        *rotary_tables(seg_row, heads),
        partner_matrix(heads),
        seg_row[:, None],
        seg_row[None, :],
    )

    def group_shares(kept, arrived, group):
        groups = lax.axis_size("dp")
        if groups > 4:
            total = (kept.astype(FULL) + arrived.astype(FULL)).astype(LOW)
            return [lax.psum_scatter(total, "dp", scatter_dimension=0, tiled=True)]
        rows = kept.shape[0] // groups

        def piece_of(place):
            terms = [
                lax.dynamic_slice_in_dim(part, place * rows, rows, 0).astype(FULL)
                for part in (kept, arrived)
            ]
            return (terms[0] + terms[1]).astype(LOW)

        return scattered(piece_of, "dp", group)

    def all_shares(share):
        if lax.axis_size("dp") > 4:
            return [lax.all_gather(share, "dp", axis=0, tiled=True)]
        return received(share, "dp")

    rows_part = length // members
    token_parts = lambda values: scattered(
        lambda place: lax.dynamic_slice_in_dim(values, place * rows_part, rows_part, 0),
        "tensor",
        member,
    )
    feature_parts = lambda values, me: scattered(
        lambda place: lax.dynamic_slice_in_dim(values, place * local, local, 1), "tensor", me
    )
    own_features = lambda values: lax.dynamic_slice_in_dim(values, member * local, local, 1)
    own_tokens = lambda values: lax.dynamic_slice_in_dim(values, member * rows_part, rows_part, 0)

    branch0, *saved0 = forward(0, section, state_in, vecs[0], biases[0], tables, owns, others)
    branch0, target_blocks = tie(branch0, target_blocks)
    terms0 = token_parts(branch0)
    target = in_order(target_blocks, member, 1)
    out0 = own_tokens(state_in).astype(FULL) + total_of(terms0) + vecs[0][5]
    state1 = lax.all_gather(out0.astype(LOW), "tensor", axis=0, tiled=True)
    branch1, *saved1 = forward(1, section, state1, vecs[1], biases[1], tables, owns, others)

    _, norm1, d_low1, sent1, kept1 = backward(
        1, section, target, state1, vecs[1], tables, saved1, owns, others
    )
    terms1 = token_parts(d_low1)
    arrived1 = swap(sent1)
    d_sum1 = total_of(terms1)
    stats1 = own_tokens(saved1[1])
    unit1 = (own_tokens(state1).astype(FULL) - stats1[:, 3:4]) * stats1[:, 4:5]
    d_in1 = own_tokens(target).astype(FULL) + stats1[:, 4:5] * (
        d_sum1
        - jnp.mean(d_sum1, axis=-1, keepdims=True)
        - unit1 * jnp.mean(d_sum1 * unit1, axis=-1, keepdims=True)
    )
    group = lax.axis_index("dp")
    share1 = total_of(group_shares(kept1, arrived1, group)).astype(LOW)
    grad0 = lax.all_gather(d_in1.astype(LOW), "tensor", axis=0, tiled=True)
    grad0, share1, branch1 = tie(grad0, share1, branch1)
    terms_out = feature_parts(branch1, member)

    all1 = all_shares(share1)
    moments0, norm0, d_low0, sent0, kept0 = backward(
        0, section, grad0, state_in, vecs[0], tables, saved0, owns, others
    )
    all1, terms_out, sent0 = tie(all1, terms_out, sent0)
    out1 = (
        own_features(state1).astype(FULL)
        + total_of(terms_out)
        + own_features(vecs[1][5:6])
    )
    arrived0 = swap(sent0)
    shares0 = group_shares(kept0, arrived0, group)

    member0, arrived0 = tie(member, arrived0)
    norm_columns = jnp.concatenate([norm0, norm1]).reshape(length, -1)
    part0 = jnp.concatenate([moments0, norm_columns], axis=1)
    part0 = part0.astype(LOW)
    terms0 = scattered(
        lambda place: jnp.concatenate(
            [lax.dynamic_slice_in_dim(d_low0, place * local, local, 1), part0], axis=1
        ),
        "tensor",
        member0,
    )
    shares0, terms0 = tie(shares0, terms0)
    d_sum0 = total_of(terms0)
    rows0 = jnp.concatenate(
        [total_of(shares0), d_sum0[:, local + 2 :].reshape(16, width // 2)]
    ).astype(LOW)
    groups = lax.axis_size("dp")
    if groups > 4:
        all0 = all_shares(rows0[:-16])
        norm_sum = lax.psum(rows0[-16:].astype(FULL), "dp")
    else:
        all0 = all_shares(rows0)
        norm_sum = pair_sum([block[-16:].astype(FULL) for block in all0])
    norm_sum = (norm_sum + swap(norm_sum)).reshape(8, width)
    norm_rows = jnp.where(first_core, norm_sum[:4], norm_sum[4:])
    part0 = d_sum0[:, local:]
    stats0 = saved0[1]
    unit0 = (own_features(state_in).astype(FULL) - stats0[:, 3:4]) * stats0[:, 4:5]
    d_in0 = own_features(grad0).astype(FULL) + stats0[:, 4:5] * (
        d_sum0[:, :local] - part0[:, :1] - unit0 * part0[:, 1:2]
    )

    arrived = [
        swap(jnp.where(first_core, high, low[: high.shape[0]])) for low, high in zip(all0, all1)
    ]
    g_down, g_out, g_up, g_qkv, small = finished(
        section,
        group,
        all0,
        all1,
        arrived,
        [
            down_weight.shape[1:],
            out_weight.shape[1:],
            up_weight.shape[1:],
            owns[0].shape,
            (SMALL_ROWS, width),
        ],
    )
    own0, own1 = own_features(state1), out1.astype(LOW)
    d_own1 = own_features(grad0)
    rows_sent = jnp.where(
        first_core,
        jnp.concatenate([own1, d_own1], axis=1),
        jnp.concatenate([own0, d_in0.astype(LOW)], axis=1),
    )
    rows_other = swap(rows_sent)
    state_other, d_other = rows_other[:, :local], rows_other[:, local:].astype(FULL)

    def both_parts(low_value, high_value, arrived):
        mine = jnp.where(first_core, low_value, high_value)
        return jnp.concatenate(
            [jnp.where(first_core, mine, arrived), jnp.where(first_core, arrived, mine)]
        )[None]

    states_out = both_parts(own0, own1, state_other)
    d_states_out = both_parts(d_in0, d_own1.astype(FULL), d_other)
    return (
        states_out,
        d_states_out,
        g_qkv.swapaxes(1, 2)[None],
        small[2:5, :local].reshape(qkv_bias.shape),
        g_out[None],
        small[0][None],
        g_up[None],
        small[1][None],
        g_down[None],
        small[0][None],
        norm_rows[0:2][None],
        norm_rows[2:4][None],
    )


def solution(mesh):
    in_specs = (
        P("dp", "tensor"),
        P("dp", "tensor"),
        P("dp", None),
        P("pipe", None, None, "tensor"),
        P("pipe", None, "tensor"),
        P("pipe", "tensor", None),
        P("pipe", None),
        P("pipe", None, "tensor"),
        P("pipe", "tensor"),
        P("pipe", "tensor", None),
        P("pipe", None),
        P("pipe", None, None),
        P("pipe", None, None),
    )
    out_specs = (
        P("pipe", "dp", "tensor"),
        P("pipe", "dp", "tensor"),
        P("pipe", None, None, "tensor"),
        P("pipe", None, "tensor"),
        P("pipe", "tensor", None),
        P("pipe", None),
        P("pipe", None, "tensor"),
        P("pipe", "tensor"),
        P("pipe", "tensor", None),
        P("pipe", None),
        P("pipe", None, None),
        P("pipe", None, None),
    )
    return jax.shard_map(body, mesh=mesh, in_specs=in_specs, out_specs=out_specs, check_vma=False)
```

```python
from functools import partial
import math
from types import SimpleNamespace

import jax
import jax.numpy as jnp
import numpy as np
from jax import lax
from jax.experimental import pallas as pl
from jax.experimental.layout import Layout, with_layout_constraint
from jax.experimental.pallas import tpu as pltpu
from jax.sharding import PartitionSpec as P

HEAD_DIM = 64
ROT = 16
SEQ_LEN = 512
EPSILON = 1e-05
SMALL_ROWS = 64
LOW = jnp.bfloat16
FULL = jnp.float32


def swap(value):
    return lax.ppermute(value, "pipe", [(0, 1), (1, 0)])


def partner(value, axis, flip):
    count = lax.axis_size(axis)
    return lax.ppermute(value, axis, [(source, source ^ flip) for source in range(count)])


def pair_sum(terms):
    while len(terms) > 1:
        terms = [first + second for first, second in zip(terms[0::2], terms[1::2])]
    return terms[0]


def total_of(terms):
    return pair_sum([term.astype(FULL) for term in terms])


def received(value, axis):
    return [value] + [partner(value, axis, flip) for flip in range(1, lax.axis_size(axis))]


def tie(*values):
    return lax.optimization_barrier(values)


def gate_kernel(indices, *refs):
    out = refs[-1]
    for position in range(out.shape[0]):
        out[position] = indices[position]


def gate(indices, *others):
    smem = pl.BlockSpec(memory_space=pltpu.SMEM)
    return pl.pallas_call(
        gate_kernel,
        out_shape=jax.ShapeDtypeStruct(indices.shape, indices.dtype),
        in_specs=[smem] + [pl.BlockSpec(memory_space=pltpu.HBM)] * len(others),
        out_specs=smem,
        compiler_params=pltpu.CompilerParams(vmem_limit_bytes=60 * 1024 * 1024),
        cost_estimate=pl.CostEstimate(flops=0, bytes_accessed=64, transcendentals=0),
    )(indices, *others)


def rows_kernel(me, *refs):
    blocks, out, sems = refs[:-2], refs[-2], refs[-1]
    rows = blocks[0].shape[0]
    copies = []
    for flip, block in enumerate(blocks):
        start = pl.multiple_of((me[0] ^ flip) * rows, 16)
        copies.append(
            pltpu.make_async_copy(block, out.at[pl.ds(start, rows), :], sems.at[flip])
        )
    for copy in copies:
        copy.start()
    for copy in copies:
        copy.wait()


def columns_kernel(me, *refs):
    blocks, out = refs[:-1], refs[-1]
    wide = blocks[0].shape[0]
    for place in range(len(blocks)):
        for flip, block in enumerate(blocks):

            @pl.when(me[0] == place ^ flip)
            def _():
                out[:, place * wide : (place + 1) * wide] = block[...].T


def in_order(blocks, me, dim):
    count = len(blocks)
    rows, wide = blocks[0].shape
    shape = (rows * count, wide) if dim == 0 else (wide, rows * count)
    space = pl.ANY if dim == 0 else pltpu.VMEM
    return pl.pallas_call(
        rows_kernel if dim == 0 else columns_kernel,
        out_shape=jax.ShapeDtypeStruct(shape, blocks[0].dtype),
        in_specs=[pl.BlockSpec(memory_space=pltpu.SMEM)]
        + [pl.BlockSpec(memory_space=space)] * count,
        out_specs=pl.BlockSpec(memory_space=pltpu.VMEM),
        scratch_shapes=[pltpu.SemaphoreType.DMA((count,))] if dim == 0 else [],
        compiler_params=pltpu.CompilerParams(vmem_limit_bytes=8 * 1024 * 1024),
        cost_estimate=pl.CostEstimate(
            flops=0, bytes_accessed=4 * rows * wide * count, transcendentals=0
        ),
    )(me[None], *blocks)


def finish_kernel(where, *refs):
    count = (len(refs) - 17) // 3
    first, second, arrived = refs[:count], refs[count : 2 * count], refs[2 * count : 3 * count]
    outs, biases = refs[3 * count : 3 * count + 4], refs[3 * count + 4 : 3 * count + 8]
    results = refs[3 * count + 8 : 3 * count + 12]
    mine, other, small, sems, out_sems = refs[3 * count + 12 : 3 * count + 17]
    down, out, up, qkv = results
    rows = mine.shape[0] // count
    half = mine.shape[1]

    def place(index):
        start = (where[1] ^ index) * rows if count > 1 else 0
        return pl.ds(pl.multiple_of(start, 16), rows)

    for layer, blocks in enumerate((first, second)):

        @pl.when(where[0] == layer)
        def _():
            for index, block in enumerate(blocks):
                pltpu.make_async_copy(
                    block.at[pl.ds(0, rows), :], mine.at[place(index), :], sems.at[index]
                ).start()

    loads = [
        pltpu.make_async_copy(block, other.at[place(index), :], sems.at[count + index])
        for index, block in enumerate(arrived)
    ]
    for load in loads:
        load.start()
    for index, block in enumerate(second):
        pltpu.make_async_copy(
            block.at[pl.ds(0, rows), :], mine.at[place(index), :], sems.at[index]
        ).wait()
    for load in loads:
        load.wait()

    own_start = pl.multiple_of(where[0] * half, half)
    other_start = pl.multiple_of((1 - where[0]) * half, half)
    parts = ((mine, pl.ds(own_start, half)), (other, pl.ds(other_start, half)))
    row = 0
    for index, result in enumerate((down, out, up)):
        for part, columns in parts:
            result[:, columns] = part[row : row + result.shape[0], :].astype(FULL)
        row += result.shape[0]
        pltpu.make_async_copy(result, outs[index], out_sems.at[index]).start()
    for which in range(qkv.shape[0]):
        for part, columns in parts:
            qkv[which, :, columns] = part[row : row + qkv.shape[1], :].astype(FULL)
        row += qkv.shape[1]
    pltpu.make_async_copy(qkv, outs[3], out_sems.at[3]).start()
    for part, columns in parts:
        small[:, columns] = part[row : row + small.shape[0], :].astype(FULL)
    down_bias, out_bias, up_bias, qkv_bias = biases
    down_bias[...] = small[0:1, :]
    out_bias[...] = small[0:1, :]
    up_bias[...] = small[1:2, :]
    qkv_bias[...] = small[2:5, : qkv_bias.shape[1]]
    for index, result in enumerate(results):
        pltpu.make_async_copy(result, outs[index], out_sems.at[index]).wait()


def finished(section, group, first, second, arrived, shapes, bias_shapes):
    hbm = pl.BlockSpec(memory_space=pltpu.HBM)
    vmem = pl.BlockSpec(memory_space=pltpu.VMEM)
    count = len(first)
    rows, half = arrived[0].shape
    return pl.pallas_call(
        finish_kernel,
        out_shape=[jax.ShapeDtypeStruct(shape, FULL) for shape in shapes + bias_shapes],
        in_specs=[pl.BlockSpec(memory_space=pltpu.SMEM)] + [hbm] * (3 * count),
        out_specs=[hbm] * len(shapes) + [vmem] * len(bias_shapes),
        scratch_shapes=[pltpu.VMEM(shape, FULL) for shape in shapes]
        + [pltpu.VMEM((rows * count, half), LOW)] * 2
        + [pltpu.VMEM((SMALL_ROWS, 2 * half), FULL)]
        + [pltpu.SemaphoreType.DMA((2 * count,)), pltpu.SemaphoreType.DMA((len(shapes),))],
        compiler_params=pltpu.CompilerParams(vmem_limit_bytes=60 * 1024 * 1024),
        cost_estimate=pl.CostEstimate(
            flops=0, bytes_accessed=12 * rows * half * count, transcendentals=0
        ),
    )(jnp.stack([section, group]), *first, *second, *arrived)


def rotary_tables(seg_row, heads):
    length = seg_row.shape[-1]
    starts = jnp.sum((seg_row[None, :] < seg_row[:, None]).astype(jnp.int32), axis=-1)
    places = jnp.arange(length, dtype=jnp.int32) - starts
    halves = ROT // 2
    freqs = jnp.exp(jnp.arange(halves, dtype=FULL) * (-2.0 * math.log(10000.0) / ROT))
    freqs = jnp.tile(jnp.concatenate([freqs, freqs, jnp.zeros(HEAD_DIM - ROT, FULL)]), heads)
    angles = places.astype(FULL)[:, None] * freqs
    lanes = jnp.arange(heads * HEAD_DIM)
    sine = jnp.where(lanes == ROT, starts.astype(FULL)[:, None], jnp.sin(angles))
    return jnp.cos(angles), sine


def partner_matrix(heads):
    matrix = np.zeros((heads * HEAD_DIM, heads * HEAD_DIM), np.float32)
    for head in range(heads):
        for lane in range(ROT // 2):
            first = head * HEAD_DIM + lane
            second = first + ROT // 2
            matrix[second, first] = -1.0
            matrix[first, second] = 1.0
    return jnp.asarray(matrix, LOW)


def product(left, right, left_dim=1, right_dim=0):
    return lax.dot_general(
        left, right, (((left_dim,), (right_dim,)), ((), ())), preferred_element_type=FULL
    )


def head_lanes(values, head):
    lanes = lax.broadcasted_iota(jnp.int32, values.shape, 1)
    return (lanes >= head * HEAD_DIM) & (lanes < (head + 1) * HEAD_DIM)


def masked_scores(queries, key_rows, starts, first_row):
    scores = product(queries, key_rows, 1, 1) * (1.0 / math.sqrt(HEAD_DIM))
    rows = first_row + lax.broadcasted_iota(jnp.int32, scores.shape, 0)
    columns = lax.broadcasted_iota(jnp.int32, scores.shape, 1)
    return jnp.where((columns >= starts) & (columns <= rows), scores, -1e30)


STEP = 32
BLOCK = 256


def steps(length, body, init):
    def at(step, carry):
        return body(pl.ds(pl.multiple_of(step * STEP, STEP), STEP), carry)

    return lax.fori_loop(0, length // STEP, at, init)


def forward_steps(ref, vecs):
    length = ref.state.shape[0]
    ref.wait("state")

    def normed(rows, carry):
        values = ref.state[rows, :].astype(FULL)
        mean = jnp.mean(values, axis=-1, keepdims=True)
        center = values - mean
        spread = lax.rsqrt(jnp.mean(center * center, axis=-1, keepdims=True) + EPSILON)
        unit = center * spread
        if ref.unit is not None:
            ref.unit[rows, :] = unit
        ref.att[rows, :] = (unit * vecs[0:1] + vecs[2:3]).astype(LOW)
        ref.mlp[rows, :] = (unit * vecs[1:2] + vecs[3:4]).astype(LOW)
        ref.stats[rows, 3:4] = mean
        ref.stats[rows, 4:5] = spread
        return carry

    steps(length, normed, 0)

    ref.wait("cosine", "sine", "w_qkv")
    for which in range(3):
        local = ref.w_qkv.shape[1]
        values = product(ref.att[...], ref.w_qkv[which], 1, 1)
        values = values + vecs[6 + which : 7 + which, :local]
        if which < 2:
            high = values.astype(LOW)
            low = (values - high.astype(FULL)).astype(LOW)
            turned = product(high, ref.matrix[...]) + product(low, ref.matrix[...])
            values = values * ref.cosine[...] + turned * ref.sine[...]
        ref.qkv[which] = values.astype(LOW)

    for start in range(0, length, BLOCK):
        rows, keys = slice(start, start + BLOCK), slice(0, start + BLOCK)
        queries = ref.qkv[0, rows, :]
        starts = ref.sine[rows, ROT : ROT + 1].astype(jnp.int32)
        found = jnp.zeros(queries.shape, FULL)
        for head in range(queries.shape[1] // HEAD_DIM):
            own = head_lanes(queries, head)
            scores = masked_scores(
                jnp.where(own, queries, jnp.zeros_like(queries)), ref.qkv[1, keys, :], starts, start
            )
            peak = jnp.max(scores, axis=-1, keepdims=True)
            exponent = jnp.exp(scores - peak)
            totals = jnp.sum(exponent, axis=-1, keepdims=True)
            ref.stats[rows, head : head + 1] = peak + jnp.log(totals)
            probs = (exponent / totals).astype(LOW)
            found = jnp.where(own, product(probs, ref.qkv[2, keys, :]), found)
        ref.mixed[rows, :] = found.astype(LOW)

    ref.wait("w_up")
    ref.wide[...] = product(ref.mlp[...], ref.w_up[...])

    def activated(rows, carry):
        values = ref.wide[rows, :] + vecs[4:5]
        share = 0.5 + 0.5 * lax.erf(values * math.sqrt(0.5))
        bell = jnp.exp(-0.5 * values * values) * (1.0 / math.sqrt(2.0 * math.pi))
        ref.gelu[rows, :] = (values * share).astype(LOW)
        ref.slope[rows, :] = (share + values * bell).astype(LOW)
        return carry

    steps(length, activated, 0)

    ref.wait("w_out", "w_down")
    branch = product(ref.mixed[...], ref.w_out[...]) + product(ref.gelu[...], ref.w_down[...])
    ref.branch[...] = branch.astype(LOW)


def backward_steps(ref, vecs):
    length, width = ref.state.shape
    fold = lambda values: jnp.sum(values.reshape(STEP // 8, 8, values.shape[1]), axis=0)
    zero = jnp.zeros((8, width), FULL)

    ref.wait("grad", "w_out")
    ref.d_mixed[...] = product(ref.grad[...], ref.w_out[...], 1, 1).astype(LOW)
    ref.wait("w_down")
    ref.wide[...] = product(ref.grad[...], ref.w_down[...], 1, 1)
    ref.wait("slope")

    def activated(rows, carry):
        values = (ref.wide[rows, :] * ref.slope[rows, :].astype(FULL)).astype(LOW)
        ref.d_act[rows, :] = values
        return carry[0] + fold(values.astype(FULL)), carry[1] + fold(ref.grad[rows, :].astype(FULL))

    act_sum, grad_sum = steps(length, activated, (zero, zero))

    ref.wait("qkv", "sine", "stats")
    ref.d_keys[...] = jnp.zeros_like(ref.d_keys)
    ref.d_values[...] = jnp.zeros_like(ref.d_values)
    for start in range(0, length, BLOCK):
        rows, keys = slice(start, start + BLOCK), slice(0, start + BLOCK)
        queries, upper = ref.qkv[0, rows, :], ref.d_mixed[rows, :]
        key_rows, value_rows = ref.qkv[1, keys, :], ref.qkv[2, keys, :]
        starts = ref.sine[rows, ROT : ROT + 1].astype(jnp.int32)
        found = jnp.zeros(queries.shape, FULL)
        for head in range(queries.shape[1] // HEAD_DIM):
            own = head_lanes(queries, head)
            clear = jnp.zeros_like(queries)
            own_queries, own_upper = jnp.where(own, queries, clear), jnp.where(own, upper, clear)
            scores = masked_scores(own_queries, key_rows, starts, start)
            probs = jnp.exp(scores - ref.stats[rows, head : head + 1])
            d_probs = product(own_upper, value_rows, 1, 1)
            middle = jnp.sum(d_probs * probs, axis=-1, keepdims=True)
            d_scores = (probs * (d_probs - middle)).astype(LOW)
            found = jnp.where(own, product(d_scores, key_rows), found)
            ref.d_keys[keys, :] += product(d_scores, own_queries, 0, 0)
            ref.d_values[keys, :] += product(probs.astype(LOW), own_upper, 0, 0)
        ref.d_queries[rows, :] = found

    ref.wait("cosine")
    scale = 1.0 / math.sqrt(HEAD_DIM)
    for which, source in enumerate((ref.d_queries, ref.d_keys)):
        values = (source[...] * scale).astype(LOW)
        turned = product(values, ref.matrix[...])
        values = values.astype(FULL) * ref.cosine[...] - turned * ref.sine[...]
        ref.proj[which] = values.astype(LOW)
    ref.proj[2] = ref.d_values[...].astype(LOW)

    ref.wait("w_up")
    ref.second[...] = product(ref.d_act[...], ref.w_up[...], 1, 1)
    ref.wait("w_qkv")
    ref.wide[...] = (
        product(ref.proj[0], ref.w_qkv[0])
        + product(ref.proj[1], ref.w_qkv[1])
        + product(ref.proj[2], ref.w_qkv[2])
    )
    ref.moments[...] = jnp.zeros_like(ref.moments)

    def joined(rows, carry):
        d_att, d_mlp, values = ref.wide[rows, :], ref.second[rows, :], ref.unit[rows, :]
        total = (d_att * vecs[0:1] + d_mlp * vecs[1:2]).astype(LOW)
        ref.d_low[rows, :] = total
        total = total.astype(FULL)
        ref.moments[rows, 0:1] = jnp.mean(total, axis=-1, keepdims=True)
        ref.moments[rows, 1:2] = jnp.mean(total * values, axis=-1, keepdims=True)
        return (
            carry[0] + fold(d_att * values),
            carry[1] + fold(d_mlp * values),
            carry[2] + fold(d_att),
            carry[3] + fold(d_mlp),
        )

    sums = steps(length, joined, (zero,) * 4)
    ref.norms[...] = jnp.concatenate([jnp.sum(rows, axis=0, keepdims=True) for rows in sums])
    ref.joined()

    ref.small[...] = jnp.zeros_like(ref.small)
    ref.small[0:1, :] = jnp.sum(grad_sum, axis=0, keepdims=True)
    ref.small[1:2, :] = jnp.sum(act_sum, axis=0, keepdims=True)
    for which in range(3):
        ref.small[2 + which : 3 + which, 0 : ref.proj.shape[2]] = jnp.sum(
            ref.proj[which].astype(FULL), axis=0, keepdims=True
        )

    ref.wait("mixed", "gelu")
    half = ref.kept.shape[1]
    for out, place, store in (
        (ref.sent, 1 - ref.section, ref.store_sent),
        (ref.kept, ref.section, ref.store_kept),
    ):
        lanes = pl.ds(pl.multiple_of(place * half, half), half)
        row = 0

        def put(left, right):
            out[row : row + left.shape[1], :] = product(left, right, 0, 0).astype(LOW)
            return row + left.shape[1]

        rows_grad = ref.grad[:, lanes]
        row = put(ref.gelu[...], rows_grad)
        row = put(ref.mixed[...], rows_grad)
        row = put(ref.mlp[...], ref.d_act[:, lanes])
        rows_att = ref.att[:, lanes]
        for which in range(ref.proj.shape[0]):
            row = put(ref.proj[which], rows_att)
        out[row : row + ref.small.shape[0], :] = ref.small[:, lanes].astype(LOW)
        store()


WEIGHTS = ("w_qkv", "w_out", "w_up", "w_down")


def layer_kernel(layer, plan, where, *refs):
    names = plan["whole"] + [name + " in" for name in plan["loaded"]]
    names += ["own " + name for name in WEIGHTS]
    names += ["other " + name for name in WEIGHTS] + plan["outs"]
    names += ["sems", "out_sems"] + list(plan["buffers"])
    table = dict(zip(names, refs, strict=True))
    ref = SimpleNamespace(unit=None)
    for name in list(plan["buffers"]) + plan["whole"]:
        setattr(ref, name, table[name])
    sems, out_sems = table["sems"], table["out_sems"]
    ref.section = where[0]
    member, group = where[1], where[2]

    loads = {}
    order = plan["loaded"][:2] + list(WEIGHTS) + plan["loaded"][2:]
    for index, name in enumerate(order):
        if name in WEIGHTS:
            copies = [
                pltpu.make_async_copy(table[kind + name], table[name], sems.at[index])
                for kind in ("own ", "other ")
            ]
            pl.when(ref.section == layer)(copies[0].start)
            pl.when(ref.section != layer)(copies[1].start)
            loads[name] = copies[0]
        else:
            loads[name] = pltpu.make_async_copy(table[name + " in"], table[name], sems.at[index])
            loads[name].start()

    def wait(*names):
        for name in names:
            load = loads.pop(name, None)
            if load is not None:
                load.wait()

    ref.wait = wait
    stores = []

    def store(source, target):
        copy = pltpu.make_async_copy(source, target, out_sems.at[len(stores)])
        copy.start()
        stores.append(copy)

    def store_pieces(source, prefix, rows):
        for flip in range(plan["members"]):
            start = pl.multiple_of((member ^ flip) * rows, 16)
            store(source.at[pl.ds(start, rows), :], table[prefix + str(flip)].at[pl.ds(0, rows), :])

    def store_quarters(source, target):
        groups = plan["groups"]
        rows = source.shape[0] // groups
        for flip in range(groups):
            start = pl.multiple_of((group ^ flip) * rows, 16)
            store(source.at[pl.ds(start, rows), :], target.at[pl.ds(flip * rows, rows), :])

    def turned(source, target):
        for start in range(0, source.shape[0], 128):
            rows = slice(start, start + 128)
            target[:, rows] = source[rows, :].T

    vecs = jnp.where(ref.section == layer, ref.own_vecs[...], ref.other_vecs[...])
    length, width = ref.state.shape
    local = width // plan["members"]

    if plan["forward"]:
        forward_steps(ref, vecs)
        if plan["backward"]:
            turned(ref.branch, ref.turned)
            store_pieces(ref.turned, "branch piece ", local)
            store(ref.stats, table["stats out"])
        else:
            store_pieces(ref.branch, "branch piece ", length // plan["members"])
            for name in ("qkv", "stats", "mixed", "gelu", "slope"):
                store(getattr(ref, name), table[name + " out"])
    elif plan["backward"]:
        ref.wait("state", "stats")

        def normed(rows, carry):
            values = ref.state[rows, :].astype(FULL) - ref.stats[rows, 3:4]
            values = values * ref.stats[rows, 4:5]
            ref.unit[rows, :] = values
            ref.att[rows, :] = (values * vecs[0:1] + vecs[2:3]).astype(LOW)
            ref.mlp[rows, :] = (values * vecs[1:2] + vecs[3:4]).astype(LOW)
            return carry

        steps(length, normed, 0)

    if plan["backward"]:

        def finish_rows():
            if plan["forward"]:
                store_pieces(ref.d_low, "d_low piece ", length // plan["members"])
                table["norms out"][...] = ref.norms[...]
                return
            turned(ref.d_low, ref.turned)
            moments = ref.moments[...].T[:16, :]
            norms = jnp.concatenate([ref.norms[...], ref.norms1[...]])
            rest = jnp.concatenate(
                [norms[:, length:], jnp.zeros((8, 2 * length - width), FULL)], axis=1
            )
            ref.extra[...] = jnp.concatenate([moments, norms[:, :length], rest]).astype(LOW)
            store_pieces(ref.turned, "d_low piece ", local)
            for flip in range(plan["members"]):
                target = table["d_low piece " + str(flip)]
                store(ref.extra, target.at[pl.ds(local, ref.extra.shape[0]), :])

        ref.joined = finish_rows
        ref.store_sent = lambda: store_quarters(ref.sent, table["sent out"])
        ref.store_kept = lambda: store_quarters(ref.kept, table["kept out"])
        backward_steps(ref, vecs)
    for copy in stores:
        copy.wait()


def run_layer(layer, where, members, groups, arrays, own_weights, other_weights, forward, backward):
    length, width = arrays["state"].shape
    local, units = own_weights[0].shape[1], own_weights[2].shape[1]
    rows = units + local + width + 3 * local + SMALL_ROWS
    shape = jax.ShapeDtypeStruct
    saved = {
        "qkv": shape((3, length, local), LOW),
        "stats": shape((length, 128), FULL),
        "mixed": shape((length, local), LOW),
        "gelu": shape((length, units), LOW),
        "slope": shape((length, units), LOW),
    }
    buffers = {name: shape(own.shape, LOW) for name, own in zip(WEIGHTS, own_weights)}
    buffers.update(saved)
    for name in ("state", "att", "mlp"):
        buffers[name] = shape((length, width), LOW)
    for name in ("cosine", "sine"):
        buffers[name] = shape((length, local), FULL)
    buffers["wide"] = shape((length, units), FULL)
    whole = ["own_vecs", "other_vecs", "matrix"]
    loaded = ["state"]
    outs, on_core = {}, []
    if forward:
        buffers["branch"] = shape((length, width), LOW)
        piece = (local, length) if backward else (length // members, width)
        for flip in range(members):
            outs["branch piece " + str(flip)] = shape(piece, LOW)
        for name in ["stats"] if backward else saved:
            outs[name + " out"] = saved[name]
    else:
        loaded.append("stats")
    if backward:
        loaded.append("grad")
        if not forward:
            loaded += ["slope", "qkv"]
            whole.append("norms1")
            buffers["extra"] = shape((32, length), LOW)
        for name in ("grad", "d_low"):
            buffers[name] = shape((length, width), LOW)
        buffers["turned"] = shape((width, length), LOW)
        buffers["unit"] = buffers["second"] = shape((length, width), FULL)
        buffers["d_act"] = shape((length, units), LOW)
        buffers["proj"] = saved["qkv"]
        buffers["small"] = shape((SMALL_ROWS, width), FULL)
        buffers["norms"] = shape((4, width), FULL)
        buffers["moments"] = shape((length, 128), FULL)
        for name in ("d_queries", "d_keys", "d_values"):
            buffers[name] = shape((length, local), FULL)
        buffers["d_mixed"] = saved["mixed"]
        piece = (length // members, width) if forward else (local + 32, length)
        for flip in range(members):
            outs["d_low piece " + str(flip)] = shape(piece, LOW)
        for name in ("sent", "kept"):
            buffers[name] = outs[name + " out"] = shape((rows, width // 2), LOW)
        if forward:
            on_core.append("norms out")
            outs["norms out"] = buffers["norms"]
    loaded += ["sine", "cosine"]
    if backward and not forward:
        loaded += ["mixed", "gelu"]
    plan = {
        "whole": whole,
        "loaded": loaded,
        "outs": list(outs),
        "buffers": buffers,
        "members": members,
        "groups": groups if groups <= 4 else 1,
        "forward": forward,
        "backward": backward,
    }
    vmem = pl.BlockSpec(memory_space=pltpu.VMEM)
    hbm = pl.BlockSpec(memory_space=pltpu.HBM)
    results = pl.pallas_call(
        partial(layer_kernel, layer, plan),
        out_shape=list(outs.values()),
        in_specs=[pl.BlockSpec(memory_space=pltpu.SMEM)]
        + [vmem] * len(whole)
        + [
            pl.BlockSpec(memory_space=pl.ANY) if name in ("state", "grad") else hbm
            for name in loaded
        ]
        + [hbm] * 8,
        out_specs=[vmem if name in on_core else hbm for name in outs],
        scratch_shapes=[
            pltpu.SemaphoreType.DMA((len(loaded) + 4,)),
            pltpu.SemaphoreType.DMA((len(outs) + 5 * members,)),
        ]
        + [pltpu.VMEM(buffer.shape, buffer.dtype) for buffer in buffers.values()],
        compiler_params=pltpu.CompilerParams(vmem_limit_bytes=60 * 1024 * 1024),
        cost_estimate=pl.CostEstimate(
            flops=(2 * forward + 4 * backward) * length * sum(own.size for own in own_weights),
            bytes_accessed=2 * sum(own.size for own in own_weights) + 12 * length * width,
            transcendentals=2 * length * units,
        ),
    )(
        where,
        *[arrays[name] for name in whole],
        *[arrays[name] for name in loaded],
        *own_weights,
        *other_weights,
    )
    return dict(zip(outs, results))


def body(
    hidden,
    cotangent,
    segments,
    qkv_weight,
    qkv_bias,
    out_weight,
    out_bias,
    up_weight,
    up_bias,
    down_weight,
    down_bias,
    norm_gain,
    norm_bias,
):
    section = lax.axis_index("pipe")
    member = lax.axis_index("tensor")
    group = lax.axis_index("dp")
    members = lax.axis_size("tensor")
    groups = lax.axis_size("dp")
    first_core = section == 0
    where = jnp.stack([section, member, group])
    length = SEQ_LEN
    width, local = qkv_weight.shape[2:]
    heads = local // HEAD_DIM

    own_rows = lambda rows: lax.dynamic_slice_in_dim(rows, section * length, length, 0)
    part = length // members
    own_tokens = lambda values: lax.dynamic_slice_in_dim(values, member * part, part, 0)
    pieces_of = lambda results, prefix: [results[prefix + str(flip)] for flip in range(members)]

    def exchanged(pieces, axis):
        return [pieces[0]] + [
            partner(piece, axis, flip) for flip, piece in enumerate(pieces) if flip > 0
        ]

    in_rows = lambda values: with_layout_constraint(values, Layout(major_to_minor=(0, 1)))

    def arriving(pieces):
        return [in_rows(term) for term in exchanged(pieces, "tensor")]

    state_in = lax.all_gather(own_rows(hidden), "tensor", axis=1, tiled=True)
    target_part, state_in = tie(own_rows(cotangent), state_in)
    target_blocks = received(target_part.T, "tensor")

    owns = [weight[0] for weight in (qkv_weight, out_weight, up_weight, down_weight)]
    owns[0] = owns[0].swapaxes(1, 2)
    others = [swap(own) for own in owns]
    vecs = jnp.concatenate(
        [
            norm_gain[0],
            norm_bias[0],
            up_bias,
            out_bias,
            jnp.pad(qkv_bias[0], ((0, 0), (0, width - local))),
            down_bias,
            jnp.zeros((6, width), FULL),
        ]
    )
    other_vecs = swap(vecs)
    out_biases = [rows[5] + rows[9] for rows in (vecs, other_vecs)]
    out_biases = [
        jnp.where(first_core, out_biases[0], out_biases[1]),
        jnp.where(first_core, out_biases[1], out_biases[0]),
    ]
    seg_row = lax.dynamic_index_in_dim(segments, section, 0, keepdims=False)
    cosine, sine = rotary_tables(seg_row, heads)
    common = {
        "own_vecs": vecs,
        "other_vecs": other_vecs,
        "matrix": partner_matrix(heads),
        "cosine": cosine,
        "sine": sine,
    }
    run = lambda layer, arrays, forward, backward: run_layer(
        layer, where, members, groups, dict(common, **arrays), owns, others, forward, backward
    )

    def quarters(kept, arrived):
        if groups > 4:
            return [(kept.astype(FULL) + arrived.astype(FULL)).astype(LOW)]
        rows = kept.shape[0] // groups
        cut = lambda values, flip: values[flip * rows : (flip + 1) * rows].astype(FULL)
        return [(cut(kept, flip) + cut(arrived, flip)).astype(LOW) for flip in range(groups)]

    def own_share(pieces):
        if groups > 4:
            return lax.psum_scatter(pieces[0], "dp", scatter_dimension=0, tiled=True)
        return total_of(exchanged(pieces, "dp")).astype(LOW)

    def all_shares(share):
        if groups > 4:
            return [lax.all_gather(share, "dp", axis=0, tiled=True)]
        return received(share, "dp")

    results0 = run(0, {"state": state_in}, True, False)
    pieces0, target_blocks = tie(pieces_of(results0, "branch piece "), target_blocks)
    terms0 = arriving(pieces0)
    target = in_order(target_blocks, member, 1)
    out0 = own_tokens(state_in).astype(FULL) + total_of(terms0) + out_biases[0]
    state1 = in_rows(lax.all_gather(in_rows(out0.astype(LOW)), "tensor", axis=0, tiled=True))

    results1 = run(1, {"state": state1, "grad": target}, True, True)
    terms1 = arriving(pieces_of(results1, "d_low piece "))
    arrived1 = swap(results1["sent out"])
    quarters1 = quarters(results1["kept out"], arrived1)
    share1 = own_share(quarters1)
    d_sum1 = total_of(terms1)
    stats1 = own_tokens(results1["stats out"])
    unit1 = (own_tokens(state1).astype(FULL) - stats1[:, 3:4]) * stats1[:, 4:5]
    d_in1 = own_tokens(target).astype(FULL) + stats1[:, 4:5] * (
        d_sum1
        - jnp.mean(d_sum1, axis=-1, keepdims=True)
        - unit1 * jnp.mean(d_sum1 * unit1, axis=-1, keepdims=True)
    )
    grad0 = in_rows(lax.all_gather(in_rows(d_in1.astype(LOW)), "tensor", axis=0, tiled=True))
    grad0, share1 = tie(grad0, share1)

    out_terms = arriving(pieces_of(results1, "branch piece "))
    all1 = all_shares(share1)
    saved0 = {name: results0[name + " out"] for name in ("qkv", "stats", "mixed", "gelu", "slope")}
    saved0.update(state=state_in, grad=grad0, norms1=results1["norms out"])
    results0 = run(0, saved0, False, True)
    all1, out_terms[1:], sent0 = tie(all1, out_terms[1:], results0["sent out"])
    arrived0 = swap(sent0)
    share0 = own_share(quarters(results0["kept out"], arrived0))
    all0 = all_shares(share0)

    zero = gate(jnp.zeros((1,), jnp.int32), share0)[0]

    def own_features(values):
        return lax.dynamic_slice_in_dim(values, member * local + zero, local, 1).T

    def late_sum(terms, start, rows):
        return total_of([lax.dynamic_slice_in_dim(term, zero + start, rows, 0) for term in terms])

    d_terms0 = arriving(pieces_of(results0, "d_low piece "))
    d_sum0 = late_sum(d_terms0, 0, local)
    extra0 = late_sum(d_terms0, local, 32)
    norm_sum = jnp.concatenate(
        [
            extra0[16:24],
            extra0[24:32, : width - length],
        ],
        axis=1,
    )
    norm_sum = norm_sum + swap(norm_sum)
    if groups > 4:
        norm_sum = lax.psum(norm_sum, "dp")
    else:
        norm_sum = pair_sum(received(norm_sum, "dp"))
    norm_rows = jnp.where(first_core, norm_sum[:4], norm_sum[4:])

    own0 = own_features(state1)
    bias1 = lax.dynamic_slice_in_dim(out_biases[1], member * local, local, 0)[:, None]
    own1 = (own0.astype(FULL) + total_of(out_terms) + bias1).astype(LOW)
    mean0, spread0 = saved0["stats"][:, 3], saved0["stats"][:, 4]
    unit0 = (own_features(state_in).astype(FULL) - mean0) * spread0
    d_own1 = own_features(grad0)
    d_own0 = d_own1.astype(FULL) + spread0 * (
        d_sum0 - extra0[0:1] - unit0 * extra0[1:2]
    )
    arrived = swap(
        jnp.where(
            first_core,
            jnp.concatenate([own1, d_own1]),
            jnp.concatenate([own0, d_own0.astype(LOW)]),
        )
    )

    def both_parts(low_value, high_value, arrived):
        mine = jnp.where(first_core, low_value, high_value)
        return jnp.concatenate(
            [jnp.where(first_core, mine, arrived), jnp.where(first_core, arrived, mine)], axis=1
        ).T[None]

    states_out = both_parts(own0, own1, arrived[:local])
    d_states_out = both_parts(d_own0, d_own1.astype(FULL), arrived[local:].astype(FULL))

    arrived = [
        swap(jnp.where(first_core, high, low)) for low, high in zip(all0, all1)
    ]
    g_down, g_out, g_up, g_qkv, b_down, b_out, b_up, b_qkv = finished(
        section,
        group,
        all0,
        all1,
        arrived,
        [
            down_weight.shape[1:],
            out_weight.shape[1:],
            up_weight.shape[1:],
            owns[0].shape,
        ],
        [(1, width), (1, width), (1, width), (3, local)],
    )
    return (
        states_out,
        d_states_out,
        g_qkv.swapaxes(1, 2)[None],
        b_qkv[None],
        g_out[None],
        b_out,
        g_up[None],
        b_up,
        g_down[None],
        b_down,
        norm_rows[0:2][None],
        norm_rows[2:4][None],
    )


def solution(mesh):
    in_specs = (
        P("dp", "tensor"),
        P("dp", "tensor"),
        P("dp", None),
        P("pipe", None, None, "tensor"),
        P("pipe", None, "tensor"),
        P("pipe", "tensor", None),
        P("pipe", None),
        P("pipe", None, "tensor"),
        P("pipe", "tensor"),
        P("pipe", "tensor", None),
        P("pipe", None),
        P("pipe", None, None),
        P("pipe", None, None),
    )
    out_specs = (
        P("pipe", "dp", "tensor"),
        P("pipe", "dp", "tensor"),
        P("pipe", None, None, "tensor"),
        P("pipe", None, "tensor"),
        P("pipe", "tensor", None),
        P("pipe", None),
        P("pipe", None, "tensor"),
        P("pipe", "tensor"),
        P("pipe", "tensor", None),
        P("pipe", None),
        P("pipe", None, None),
        P("pipe", None, None),
    )
    return jax.shard_map(body, mesh=mesh, in_specs=in_specs, out_specs=out_specs, check_vma=False)
```

```python
from functools import partial
import math
from types import SimpleNamespace

import jax
import jax.numpy as jnp
import numpy as np
from jax import lax
from jax.experimental import pallas as pl
from jax.experimental.layout import Layout, with_layout_constraint
from jax.experimental.pallas import tpu as pltpu
from jax.sharding import PartitionSpec as P

HEAD_DIM = 64
ROT = 16
SEQ_LEN = 512
EPSILON = 1e-05
SMALL_ROWS = 64
PIPE, TENSOR, DP = "pipe", "tensor", "dp"
LOW = jnp.bfloat16
FULL = jnp.float32


def swap(value):
    return lax.ppermute(value, PIPE, [(0, 1), (1, 0)])


def partner(value, axis, flip):
    count = lax.axis_size(axis)
    return lax.ppermute(value, axis, [(source, source ^ flip) for source in range(count)])


def pair_sum(terms):
    while len(terms) > 1:
        terms = [first + second for first, second in zip(terms[0::2], terms[1::2])]
    return terms[0]


def total_of(terms):
    return pair_sum([term.astype(FULL) for term in terms])


def received(value, axis):
    return [value] + [partner(value, axis, flip) for flip in range(1, lax.axis_size(axis))]


def tie(*values):
    return lax.optimization_barrier(values)


def gate_kernel(indices, *refs):
    out = refs[-1]
    for position in range(out.shape[0]):
        out[position] = indices[position]


def gate(indices, *others):
    smem = pl.BlockSpec(memory_space=pltpu.SMEM)
    return pl.pallas_call(
        gate_kernel,
        out_shape=jax.ShapeDtypeStruct(indices.shape, indices.dtype),
        in_specs=[smem] + [pl.BlockSpec(memory_space=pltpu.HBM)] * len(others),
        out_specs=smem,
        compiler_params=pltpu.CompilerParams(vmem_limit_bytes=60 * 1024 * 1024),
        cost_estimate=pl.CostEstimate(flops=0, bytes_accessed=64, transcendentals=0),
    )(indices, *others)


def rows_kernel(me, *refs):
    blocks, out, sems = refs[:-2], refs[-2], refs[-1]
    rows = blocks[0].shape[0]
    copies = []
    for flip, block in enumerate(blocks):
        start = pl.multiple_of((me[0] ^ flip) * rows, 16)
        copies.append(
            pltpu.make_async_copy(block, out.at[pl.ds(start, rows), :], sems.at[flip])
        )
    for copy in copies:
        copy.start()
    for copy in copies:
        copy.wait()


def columns_kernel(me, *refs):
    blocks, out = refs[:-1], refs[-1]
    wide = blocks[0].shape[0]
    for place in range(len(blocks)):
        for flip, block in enumerate(blocks):

            @pl.when(me[0] == place ^ flip)
            def _():
                out[:, place * wide : (place + 1) * wide] = block[...].T


def in_order(blocks, me, dim):
    count = len(blocks)
    rows, wide = blocks[0].shape
    shape = (rows * count, wide) if dim == 0 else (wide, rows * count)
    space = pl.ANY if dim == 0 else pltpu.VMEM
    return pl.pallas_call(
        rows_kernel if dim == 0 else columns_kernel,
        out_shape=jax.ShapeDtypeStruct(shape, blocks[0].dtype),
        in_specs=[pl.BlockSpec(memory_space=pltpu.SMEM)]
        + [pl.BlockSpec(memory_space=space)] * count,
        out_specs=pl.BlockSpec(memory_space=pltpu.VMEM),
        scratch_shapes=[pltpu.SemaphoreType.DMA((count,))] if dim == 0 else [],
        compiler_params=pltpu.CompilerParams(vmem_limit_bytes=8 * 1024 * 1024),
        cost_estimate=pl.CostEstimate(
            flops=0, bytes_accessed=4 * rows * wide * count, transcendentals=0
        ),
    )(me[None], *blocks)


def finish_kernel(where, *refs):
    count = (len(refs) - 17) // 3
    first, second, arrived = refs[:count], refs[count : 2 * count], refs[2 * count : 3 * count]
    outs, biases = refs[3 * count : 3 * count + 4], refs[3 * count + 4 : 3 * count + 8]
    results = refs[3 * count + 8 : 3 * count + 12]
    mine, other, small, sems, out_sems = refs[3 * count + 12 : 3 * count + 17]
    down, out, up, qkv = results
    rows = mine.shape[0] // count
    half = mine.shape[1]

    def place(index):
        start = (where[1] ^ index) * rows if count > 1 else 0
        return pl.ds(pl.multiple_of(start, 16), rows)

    for layer, blocks in enumerate((first, second)):

        @pl.when(where[0] == layer)
        def _():
            for index, block in enumerate(blocks):
                pltpu.make_async_copy(
                    block.at[pl.ds(0, rows), :], mine.at[place(index), :], sems.at[index]
                ).start()

    loads = [
        pltpu.make_async_copy(block, other.at[place(index), :], sems.at[count + index])
        for index, block in enumerate(arrived)
    ]
    for load in loads:
        load.start()
    for index, block in enumerate(second):
        pltpu.make_async_copy(
            block.at[pl.ds(0, rows), :], mine.at[place(index), :], sems.at[index]
        ).wait()
    for load in loads:
        load.wait()

    own_start = pl.multiple_of(where[0] * half, half)
    other_start = pl.multiple_of((1 - where[0]) * half, half)
    parts = ((mine, pl.ds(own_start, half)), (other, pl.ds(other_start, half)))
    row = 0
    for index, result in enumerate((down, out, up)):
        for part, columns in parts:
            result[:, columns] = part[row : row + result.shape[0], :].astype(FULL)
        row += result.shape[0]
        pltpu.make_async_copy(result, outs[index], out_sems.at[index]).start()
    for which in range(qkv.shape[0]):
        for part, columns in parts:
            qkv[which, :, columns] = part[row : row + qkv.shape[1], :].astype(FULL)
        row += qkv.shape[1]
    pltpu.make_async_copy(qkv, outs[3], out_sems.at[3]).start()
    for part, columns in parts:
        small[:, columns] = part[row : row + small.shape[0], :].astype(FULL)
    down_bias, out_bias, up_bias, qkv_bias = biases
    down_bias[...] = small[0:1, :]
    out_bias[...] = small[0:1, :]
    up_bias[...] = small[1:2, :]
    qkv_bias[...] = small[2:5, : qkv_bias.shape[1]]
    for index, result in enumerate(results):
        pltpu.make_async_copy(result, outs[index], out_sems.at[index]).wait()


def finished(section, group, first, second, arrived, shapes, bias_shapes):
    hbm = pl.BlockSpec(memory_space=pltpu.HBM)
    vmem = pl.BlockSpec(memory_space=pltpu.VMEM)
    count = len(first)
    rows, half = arrived[0].shape
    return pl.pallas_call(
        finish_kernel,
        out_shape=[jax.ShapeDtypeStruct(shape, FULL) for shape in shapes + bias_shapes],
        in_specs=[pl.BlockSpec(memory_space=pltpu.SMEM)] + [hbm] * (3 * count),
        out_specs=[hbm] * len(shapes) + [vmem] * len(bias_shapes),
        scratch_shapes=[pltpu.VMEM(shape, FULL) for shape in shapes]
        + [pltpu.VMEM((rows * count, half), LOW)] * 2
        + [pltpu.VMEM((SMALL_ROWS, 2 * half), FULL)]
        + [pltpu.SemaphoreType.DMA((2 * count,)), pltpu.SemaphoreType.DMA((len(shapes),))],
        compiler_params=pltpu.CompilerParams(vmem_limit_bytes=60 * 1024 * 1024),
        cost_estimate=pl.CostEstimate(
            flops=0, bytes_accessed=12 * rows * half * count, transcendentals=0
        ),
    )(jnp.stack([section, group]), *first, *second, *arrived)


def rotary_tables(seg_row, heads):
    length = seg_row.shape[-1]
    starts = jnp.sum((seg_row[None, :] < seg_row[:, None]).astype(jnp.int32), axis=-1)
    places = jnp.arange(length, dtype=jnp.int32) - starts
    halves = ROT // 2
    freqs = jnp.exp(jnp.arange(halves, dtype=FULL) * (-2.0 * math.log(10000.0) / ROT))
    freqs = jnp.tile(jnp.concatenate([freqs, freqs, jnp.zeros(HEAD_DIM - ROT, FULL)]), heads)
    angles = places.astype(FULL)[:, None] * freqs
    lanes = jnp.arange(heads * HEAD_DIM)
    sine = jnp.where(lanes == ROT, starts.astype(FULL)[:, None], jnp.sin(angles))
    return jnp.cos(angles), sine


def partner_matrix(heads):
    matrix = np.zeros((heads * HEAD_DIM, heads * HEAD_DIM), np.float32)
    for head in range(heads):
        for lane in range(ROT // 2):
            first = head * HEAD_DIM + lane
            second = first + ROT // 2
            matrix[second, first] = -1.0
            matrix[first, second] = 1.0
    return jnp.asarray(matrix, LOW)


def product(left, right, left_dim=1, right_dim=0):
    return lax.dot_general(
        left, right, (((left_dim,), (right_dim,)), ((), ())), preferred_element_type=FULL
    )


def head_lanes(values, head):
    lanes = lax.broadcasted_iota(jnp.int32, values.shape, 1)
    return (lanes >= head * HEAD_DIM) & (lanes < (head + 1) * HEAD_DIM)


def masked_scores(queries, key_rows, starts, first_row):
    scores = product(queries, key_rows, 1, 1) * (1.0 / math.sqrt(HEAD_DIM))
    rows = first_row + lax.broadcasted_iota(jnp.int32, scores.shape, 0)
    columns = lax.broadcasted_iota(jnp.int32, scores.shape, 1)
    return jnp.where((columns >= starts) & (columns <= rows), scores, -1e30)


STEP = 512
BLOCK = 512


def steps(length, body, init):
    def at(step, carry):
        return body(pl.ds(pl.multiple_of(step * STEP, STEP), STEP), carry)

    return lax.fori_loop(0, length // STEP, at, init)


def forward_steps(ref, vecs):
    length = ref.state.shape[0]
    ref.wait("state")

    def normed(rows, carry):
        values = ref.state[rows, :].astype(FULL)
        mean = jnp.mean(values, axis=-1, keepdims=True)
        center = values - mean
        spread = lax.rsqrt(jnp.mean(center * center, axis=-1, keepdims=True) + EPSILON)
        unit = center * spread
        if ref.unit is not None:
            ref.unit[rows, :] = unit
        ref.att[rows, :] = (unit * vecs[0:1] + vecs[2:3]).astype(LOW)
        ref.mlp[rows, :] = (unit * vecs[1:2] + vecs[3:4]).astype(LOW)
        ref.stats[rows, 3:4] = mean
        ref.stats[rows, 4:5] = spread
        return carry

    steps(length, normed, 0)

    ref.wait("cosine", "sine", "w_qkv")
    for which in range(3):
        local = ref.w_qkv.shape[1]
        values = product(ref.att[...], ref.w_qkv[which], 1, 1)
        values = values + vecs[6 + which : 7 + which, :local]
        if which < 2:
            high = values.astype(LOW)
            low = (values - high.astype(FULL)).astype(LOW)
            turned = product(high, ref.matrix[...]) + product(low, ref.matrix[...])
            values = values * ref.cosine[...] + turned * ref.sine[...]
        ref.qkv[which] = values.astype(LOW)

    for start in range(0, length, BLOCK):
        rows, keys = slice(start, start + BLOCK), slice(0, start + BLOCK)
        queries = ref.qkv[0, rows, :]
        starts = ref.sine[rows, ROT : ROT + 1].astype(jnp.int32)
        found = jnp.zeros(queries.shape, FULL)
        for head in range(queries.shape[1] // HEAD_DIM):
            own = head_lanes(queries, head)
            scores = masked_scores(
                jnp.where(own, queries, jnp.zeros_like(queries)), ref.qkv[1, keys, :], starts, start
            )
            peak = jnp.max(scores, axis=-1, keepdims=True)
            exponent = jnp.exp(scores - peak)
            totals = jnp.sum(exponent, axis=-1, keepdims=True)
            ref.stats[rows, head : head + 1] = peak + jnp.log(totals)
            probs = (exponent / totals).astype(LOW)
            found = jnp.where(own, product(probs, ref.qkv[2, keys, :]), found)
        ref.mixed[rows, :] = found.astype(LOW)

    ref.wait("w_up")
    ref.wide[...] = product(ref.mlp[...], ref.w_up[...])

    def activated(rows, carry):
        values = ref.wide[rows, :] + vecs[4:5]
        share = 0.5 + 0.5 * lax.erf(values * math.sqrt(0.5))
        bell = jnp.exp(-0.5 * values * values) * (1.0 / math.sqrt(2.0 * math.pi))
        ref.gelu[rows, :] = (values * share).astype(LOW)
        ref.slope[rows, :] = (share + values * bell).astype(LOW)
        return carry

    steps(length, activated, 0)

    ref.wait("w_out", "w_down")
    branch = product(ref.mixed[...], ref.w_out[...]) + product(ref.gelu[...], ref.w_down[...])
    ref.branch[...] = branch.astype(LOW)


def backward_steps(ref, vecs):
    length, width = ref.state.shape
    fold = lambda values: jnp.sum(values.reshape(STEP // 8, 8, values.shape[1]), axis=0)
    zero = jnp.zeros((8, width), FULL)

    ref.wait("grad", "w_out")
    ref.d_mixed[...] = product(ref.grad[...], ref.w_out[...], 1, 1).astype(LOW)
    ref.wait("w_down")
    ref.wide[...] = product(ref.grad[...], ref.w_down[...], 1, 1)
    ref.wait("slope")

    def activated(rows, carry):
        values = (ref.wide[rows, :] * ref.slope[rows, :].astype(FULL)).astype(LOW)
        ref.d_act[rows, :] = values
        return carry[0] + fold(values.astype(FULL)), carry[1] + fold(ref.grad[rows, :].astype(FULL))

    act_sum, grad_sum = steps(length, activated, (zero, zero))

    ref.wait("qkv", "sine", "stats")
    ref.d_keys[...] = jnp.zeros_like(ref.d_keys)
    ref.d_values[...] = jnp.zeros_like(ref.d_values)
    for start in range(0, length, BLOCK):
        rows, keys = slice(start, start + BLOCK), slice(0, start + BLOCK)
        queries, upper = ref.qkv[0, rows, :], ref.d_mixed[rows, :]
        key_rows, value_rows = ref.qkv[1, keys, :], ref.qkv[2, keys, :]
        starts = ref.sine[rows, ROT : ROT + 1].astype(jnp.int32)
        found = jnp.zeros(queries.shape, FULL)
        for head in range(queries.shape[1] // HEAD_DIM):
            own = head_lanes(queries, head)
            clear = jnp.zeros_like(queries)
            own_queries, own_upper = jnp.where(own, queries, clear), jnp.where(own, upper, clear)
            scores = masked_scores(own_queries, key_rows, starts, start)
            probs = jnp.exp(scores - ref.stats[rows, head : head + 1])
            d_probs = product(own_upper, value_rows, 1, 1)
            middle = jnp.sum(d_probs * probs, axis=-1, keepdims=True)
            d_scores = (probs * (d_probs - middle)).astype(LOW)
            found = jnp.where(own, product(d_scores, key_rows), found)
            ref.d_keys[keys, :] += product(d_scores, own_queries, 0, 0)
            ref.d_values[keys, :] += product(probs.astype(LOW), own_upper, 0, 0)
        ref.d_queries[rows, :] = found

    ref.wait("cosine")
    scale = 1.0 / math.sqrt(HEAD_DIM)
    for which, source in enumerate((ref.d_queries, ref.d_keys)):
        values = (source[...] * scale).astype(LOW)
        turned = product(values, ref.matrix[...])
        values = values.astype(FULL) * ref.cosine[...] - turned * ref.sine[...]
        ref.proj[which] = values.astype(LOW)
    ref.proj[2] = ref.d_values[...].astype(LOW)

    ref.wait("w_up")
    ref.second[...] = product(ref.d_act[...], ref.w_up[...], 1, 1)
    ref.wait("w_qkv")
    ref.wide[...] = (
        product(ref.proj[0], ref.w_qkv[0])
        + product(ref.proj[1], ref.w_qkv[1])
        + product(ref.proj[2], ref.w_qkv[2])
    )
    ref.moments[...] = jnp.zeros_like(ref.moments)

    def joined(rows, carry):
        d_att, d_mlp, values = ref.wide[rows, :], ref.second[rows, :], ref.unit[rows, :]
        total = (d_att * vecs[0:1] + d_mlp * vecs[1:2]).astype(LOW)
        ref.d_low[rows, :] = total
        total = total.astype(FULL)
        ref.moments[rows, 0:1] = jnp.mean(total, axis=-1, keepdims=True)
        ref.moments[rows, 1:2] = jnp.mean(total * values, axis=-1, keepdims=True)
        return (
            carry[0] + fold(d_att * values),
            carry[1] + fold(d_mlp * values),
            carry[2] + fold(d_att),
            carry[3] + fold(d_mlp),
        )

    sums = steps(length, joined, (zero,) * 4)
    ref.norms[...] = jnp.concatenate([jnp.sum(rows, axis=0, keepdims=True) for rows in sums])
    ref.joined()

    ref.small[...] = jnp.zeros_like(ref.small)
    ref.small[0:1, :] = jnp.sum(grad_sum, axis=0, keepdims=True)
    ref.small[1:2, :] = jnp.sum(act_sum, axis=0, keepdims=True)
    for which in range(3):
        ref.small[2 + which : 3 + which, 0 : ref.proj.shape[2]] = jnp.sum(
            ref.proj[which].astype(FULL), axis=0, keepdims=True
        )

    ref.wait("mixed", "gelu")
    half = ref.kept.shape[1]
    for out, place, store in (
        (ref.sent, 1 - ref.section, ref.store_sent),
        (ref.kept, ref.section, ref.store_kept),
    ):
        lanes = pl.ds(pl.multiple_of(place * half, half), half)
        row = 0

        def put(left, right):
            out[row : row + left.shape[1], :] = product(left, right, 0, 0).astype(LOW)
            return row + left.shape[1]

        rows_grad = ref.grad[:, lanes]
        row = put(ref.gelu[...], rows_grad)
        row = put(ref.mixed[...], rows_grad)
        row = put(ref.mlp[...], ref.d_act[:, lanes])
        rows_att = ref.att[:, lanes]
        for which in range(ref.proj.shape[0]):
            row = put(ref.proj[which], rows_att)
        out[row : row + ref.small.shape[0], :] = ref.small[:, lanes].astype(LOW)
        store()


WEIGHTS = ("w_qkv", "w_out", "w_up", "w_down")


def layer_kernel(layer, plan, where, *refs):
    names = plan["whole"] + [name + " in" for name in plan["loaded"]]
    names += ["own " + name for name in WEIGHTS]
    names += ["other " + name for name in WEIGHTS] + plan["outs"]
    names += ["sems", "out_sems"] + list(plan["buffers"])
    table = dict(zip(names, refs, strict=True))
    ref = SimpleNamespace(unit=None)
    for name in list(plan["buffers"]) + plan["whole"]:
        setattr(ref, name, table[name])
    sems, out_sems = table["sems"], table["out_sems"]
    ref.section = where[0]
    member, group = where[1], where[2]

    loads = {}
    order = plan["loaded"][:2] + list(WEIGHTS) + plan["loaded"][2:]
    for index, name in enumerate(order):
        if name in WEIGHTS:
            copies = [
                pltpu.make_async_copy(table[kind + name], table[name], sems.at[index])
                for kind in ("own ", "other ")
            ]
            pl.when(ref.section == layer)(copies[0].start)
            pl.when(ref.section != layer)(copies[1].start)
            loads[name] = copies[0]
        else:
            loads[name] = pltpu.make_async_copy(table[name + " in"], table[name], sems.at[index])
            loads[name].start()

    def wait(*names):
        for name in names:
            load = loads.pop(name, None)
            if load is not None:
                load.wait()

    ref.wait = wait
    stores = []

    def store(source, target):
        copy = pltpu.make_async_copy(source, target, out_sems.at[len(stores)])
        copy.start()
        stores.append(copy)

    def store_pieces(source, prefix, rows):
        for flip in range(plan["members"]):
            start = pl.multiple_of((member ^ flip) * rows, 16)
            store(source.at[pl.ds(start, rows), :], table[prefix + str(flip)].at[pl.ds(0, rows), :])

    def store_quarters(source, target):
        groups = plan["groups"]
        rows = source.shape[0] // groups
        for flip in range(groups):
            start = pl.multiple_of((group ^ flip) * rows, 16)
            store(source.at[pl.ds(start, rows), :], target.at[pl.ds(flip * rows, rows), :])

    def turned(source, target):
        for start in range(0, source.shape[0], 128):
            rows = slice(start, start + 128)
            target[:, rows] = source[rows, :].T

    vecs = jnp.where(ref.section == layer, ref.own_vecs[...], ref.other_vecs[...])
    length, width = ref.state.shape
    local = width // plan["members"]

    if plan["forward"]:
        forward_steps(ref, vecs)
        if plan["backward"]:
            turned(ref.branch, ref.turned)
            store_pieces(ref.turned, "out ", local)
            store(ref.stats, table["stats out"])
        else:
            store_pieces(ref.branch, "out ", length // plan["members"])
            for name in ("qkv", "stats", "mixed", "gelu", "slope"):
                store(getattr(ref, name), table[name + " out"])
    elif plan["backward"]:
        ref.wait("state", "stats")

        def normed(rows, carry):
            values = ref.state[rows, :].astype(FULL) - ref.stats[rows, 3:4]
            values = values * ref.stats[rows, 4:5]
            ref.unit[rows, :] = values
            ref.att[rows, :] = (values * vecs[0:1] + vecs[2:3]).astype(LOW)
            ref.mlp[rows, :] = (values * vecs[1:2] + vecs[3:4]).astype(LOW)
            return carry

        steps(length, normed, 0)

    if plan["backward"]:

        def finish_rows():
            if plan["forward"]:
                store_pieces(ref.d_low, "low ", length // plan["members"])
                table["norms out"][...] = ref.norms[...]
                return
            turned(ref.d_low, ref.turned)
            moments = ref.moments[...].T[:16, :]
            norms = jnp.concatenate([ref.norms[...], ref.norms1[...]])
            rest = jnp.concatenate(
                [norms[:, length:], jnp.zeros((8, 2 * length - width), FULL)], axis=1
            )
            ref.extra[...] = jnp.concatenate([moments, norms[:, :length], rest]).astype(LOW)
            store_pieces(ref.turned, "low ", local)
            for flip in range(plan["members"]):
                target = table["low " + str(flip)]
                store(ref.extra, target.at[pl.ds(local, ref.extra.shape[0]), :])

        ref.joined = finish_rows
        ref.store_sent = lambda: store_quarters(ref.sent, table["sent out"])
        ref.store_kept = lambda: store_quarters(ref.kept, table["kept out"])
        backward_steps(ref, vecs)
    for copy in stores:
        copy.wait()


def run_layer(layer, where, members, groups, arrays, own_weights, other_weights, forward, backward):
    length, width = arrays["state"].shape
    local, units = own_weights[0].shape[1], own_weights[2].shape[1]
    rows = units + local + width + 3 * local + SMALL_ROWS
    shape = jax.ShapeDtypeStruct
    saved = {
        "qkv": shape((3, length, local), LOW),
        "stats": shape((length, 128), FULL),
        "mixed": shape((length, local), LOW),
        "gelu": shape((length, units), LOW),
        "slope": shape((length, units), LOW),
    }
    buffers = {name: shape(own.shape, LOW) for name, own in zip(WEIGHTS, own_weights)}
    buffers.update(saved)
    for name in ("state", "att", "mlp"):
        buffers[name] = shape((length, width), LOW)
    for name in ("cosine", "sine"):
        buffers[name] = shape((length, local), FULL)
    buffers["wide"] = shape((length, units), FULL)
    whole = ["own_vecs", "other_vecs", "matrix"]
    loaded = ["state"]
    outs, on_core = {}, []
    if forward:
        buffers["branch"] = shape((length, width), LOW)
        piece = (local, length) if backward else (length // members, width)
        for flip in range(members):
            outs["out " + str(flip)] = shape(piece, LOW)
        for name in ["stats"] if backward else saved:
            outs[name + " out"] = saved[name]
    else:
        loaded.append("stats")
    if backward:
        loaded.append("grad")
        if not forward:
            loaded += ["slope", "qkv"]
            whole.append("norms1")
            buffers["extra"] = shape((32, length), LOW)
        for name in ("grad", "d_low"):
            buffers[name] = shape((length, width), LOW)
        buffers["turned"] = shape((width, length), LOW)
        buffers["unit"] = buffers["second"] = shape((length, width), FULL)
        buffers["d_act"] = shape((length, units), LOW)
        buffers["proj"] = saved["qkv"]
        buffers["small"] = shape((SMALL_ROWS, width), FULL)
        buffers["norms"] = shape((4, width), FULL)
        buffers["moments"] = shape((length, 128), FULL)
        for name in ("d_queries", "d_keys", "d_values"):
            buffers[name] = shape((length, local), FULL)
        buffers["d_mixed"] = saved["mixed"]
        piece = (length // members, width) if forward else (local + 32, length)
        for flip in range(members):
            outs["low " + str(flip)] = shape(piece, LOW)
        for name in ("sent", "kept"):
            buffers[name] = outs[name + " out"] = shape((rows, width // 2), LOW)
        if forward:
            on_core.append("norms out")
            outs["norms out"] = buffers["norms"]
    loaded += ["sine", "cosine"]
    if backward and not forward:
        loaded += ["mixed", "gelu"]
    plan = {
        "whole": whole,
        "loaded": loaded,
        "outs": list(outs),
        "buffers": buffers,
        "members": members,
        "groups": groups if groups <= 4 else 1,
        "forward": forward,
        "backward": backward,
    }
    vmem = pl.BlockSpec(memory_space=pltpu.VMEM)
    hbm = pl.BlockSpec(memory_space=pltpu.HBM)
    results = pl.pallas_call(
        partial(layer_kernel, layer, plan),
        out_shape=list(outs.values()),
        in_specs=[pl.BlockSpec(memory_space=pltpu.SMEM)]
        + [vmem] * len(whole)
        + [
            pl.BlockSpec(memory_space=pl.ANY) if name in ("state", "grad") else hbm
            for name in loaded
        ]
        + [hbm] * 8,
        out_specs=[vmem if name in on_core else hbm for name in outs],
        scratch_shapes=[
            pltpu.SemaphoreType.DMA((len(loaded) + 4,)),
            pltpu.SemaphoreType.DMA((len(outs) + 5 * members,)),
        ]
        + [pltpu.VMEM(buffer.shape, buffer.dtype) for buffer in buffers.values()],
        compiler_params=pltpu.CompilerParams(vmem_limit_bytes=60 * 1024 * 1024),
        cost_estimate=pl.CostEstimate(
            flops=(2 * forward + 4 * backward) * length * sum(own.size for own in own_weights),
            bytes_accessed=2 * sum(own.size for own in own_weights) + 12 * length * width,
            transcendentals=2 * length * units,
        ),
    )(
        where,
        *[arrays[name] for name in whole],
        *[arrays[name] for name in loaded],
        *own_weights,
        *other_weights,
    )
    return dict(zip(outs, results))


def body(
    hidden,
    cotangent,
    segments,
    qkv_weight,
    qkv_bias,
    out_weight,
    out_bias,
    up_weight,
    up_bias,
    down_weight,
    down_bias,
    norm_gain,
    norm_bias,
):
    section = lax.axis_index(PIPE)
    member = lax.axis_index(TENSOR)
    group = lax.axis_index(DP)
    members = lax.axis_size(TENSOR)
    groups = lax.axis_size(DP)
    first_core = section == 0
    where = jnp.stack([section, member, group])
    length = SEQ_LEN
    width, local = qkv_weight.shape[2:]
    heads = local // HEAD_DIM

    own_rows = lambda rows: lax.dynamic_slice_in_dim(rows, section * length, length, 0)
    part = length // members
    own_tokens = lambda values: lax.dynamic_slice_in_dim(values, member * part, part, 0)
    pieces_of = lambda results, prefix: [results[prefix + str(flip)] for flip in range(members)]

    def exchanged(pieces, axis):
        return [pieces[0]] + [
            partner(piece, axis, flip) for flip, piece in enumerate(pieces) if flip > 0
        ]

    in_rows = lambda values: with_layout_constraint(values, Layout(major_to_minor=(0, 1)))

    def arriving(pieces):
        return [in_rows(term) for term in exchanged(pieces, TENSOR)]

    state_in = lax.all_gather(own_rows(hidden), TENSOR, axis=1, tiled=True)
    target_part, state_in = tie(own_rows(cotangent), state_in)
    target_blocks = received(target_part.T, TENSOR)

    owns = [weight[0] for weight in (qkv_weight, out_weight, up_weight, down_weight)]
    owns[0] = owns[0].swapaxes(1, 2)
    others = [swap(own) for own in owns]
    vecs = jnp.concatenate(
        [
            norm_gain[0],
            norm_bias[0],
            up_bias,
            out_bias,
            jnp.pad(qkv_bias[0], ((0, 0), (0, width - local))),
            down_bias,
            jnp.zeros((6, width), FULL),
        ]
    )
    other_vecs = swap(vecs)
    out_biases = [rows[5] + rows[9] for rows in (vecs, other_vecs)]
    out_biases = [
        jnp.where(first_core, out_biases[0], out_biases[1]),
        jnp.where(first_core, out_biases[1], out_biases[0]),
    ]
    seg_row = lax.dynamic_index_in_dim(segments, section, 0, keepdims=False)
    cosine, sine = rotary_tables(seg_row, heads)
    common = {
        "own_vecs": vecs,
        "other_vecs": other_vecs,
        "matrix": partner_matrix(heads),
        "cosine": cosine,
        "sine": sine,
    }
    run = lambda layer, arrays, forward, backward: run_layer(
        layer, where, members, groups, dict(common, **arrays), owns, others, forward, backward
    )

    def quarters(kept, arrived):
        if groups > 4:
            return [(kept.astype(FULL) + arrived.astype(FULL)).astype(LOW)]
        rows = kept.shape[0] // groups
        cut = lambda values, flip: values[flip * rows : (flip + 1) * rows].astype(FULL)
        return [(cut(kept, flip) + cut(arrived, flip)).astype(LOW) for flip in range(groups)]

    def own_share(pieces):
        if groups > 4:
            return lax.psum_scatter(pieces[0], DP, scatter_dimension=0, tiled=True)
        return total_of(exchanged(pieces, DP)).astype(LOW)

    def all_shares(share):
        if groups > 4:
            return [lax.all_gather(share, DP, axis=0, tiled=True)]
        return received(share, DP)

    results0 = run(0, {"state": state_in}, True, False)
    pieces0, target_blocks = tie(pieces_of(results0, "out "), target_blocks)
    terms0 = arriving(pieces0)
    target = in_order(target_blocks, member, 1)
    out0 = own_tokens(state_in).astype(FULL) + total_of(terms0) + out_biases[0]
    state1 = in_rows(lax.all_gather(in_rows(out0.astype(LOW)), TENSOR, axis=0, tiled=True))

    results1 = run(1, {"state": state1, "grad": target}, True, True)
    terms1 = arriving(pieces_of(results1, "low "))
    arrived1 = swap(results1["sent out"])
    quarters1 = quarters(results1["kept out"], arrived1)
    share1 = own_share(quarters1)
    d_sum1 = total_of(terms1)
    stats1 = own_tokens(results1["stats out"])
    unit1 = (own_tokens(state1).astype(FULL) - stats1[:, 3:4]) * stats1[:, 4:5]
    d_in1 = own_tokens(target).astype(FULL) + stats1[:, 4:5] * (
        d_sum1
        - jnp.mean(d_sum1, axis=-1, keepdims=True)
        - unit1 * jnp.mean(d_sum1 * unit1, axis=-1, keepdims=True)
    )
    grad0 = in_rows(lax.all_gather(in_rows(d_in1.astype(LOW)), TENSOR, axis=0, tiled=True))
    grad0, share1 = tie(grad0, share1)

    out_terms = arriving(pieces_of(results1, "out "))
    all1 = all_shares(share1)
    saved0 = {name: results0[name + " out"] for name in ("qkv", "stats", "mixed", "gelu", "slope")}
    saved0.update(state=state_in, grad=grad0, norms1=results1["norms out"])
    results0 = run(0, saved0, False, True)
    all1, out_terms[1:], sent0 = tie(all1, out_terms[1:], results0["sent out"])
    arrived0 = swap(sent0)
    share0 = own_share(quarters(results0["kept out"], arrived0))
    all0 = all_shares(share0)

    zero = gate(jnp.zeros((1,), jnp.int32), share0)[0]

    def own_features(values):
        return lax.dynamic_slice_in_dim(values, member * local + zero, local, 1).T

    def late_sum(terms, start, rows):
        return total_of([lax.dynamic_slice_in_dim(term, zero + start, rows, 0) for term in terms])

    d_terms0 = arriving(pieces_of(results0, "low "))
    d_sum0 = late_sum(d_terms0, 0, local)
    extra0 = late_sum(d_terms0, local, 32)
    norm_sum = jnp.concatenate(
        [
            extra0[16:24],
            extra0[24:32, : width - length],
        ],
        axis=1,
    )
    norm_sum = norm_sum + swap(norm_sum)
    if groups > 4:
        norm_sum = lax.psum(norm_sum, DP)
    else:
        norm_sum = pair_sum(received(norm_sum, DP))
    norm_rows = jnp.where(first_core, norm_sum[:4], norm_sum[4:])

    own0 = own_features(state1)
    bias1 = lax.dynamic_slice_in_dim(out_biases[1], member * local, local, 0)[:, None]
    own1 = (own0.astype(FULL) + total_of(out_terms) + bias1).astype(LOW)
    mean0, spread0 = saved0["stats"][:, 3], saved0["stats"][:, 4]
    unit0 = (own_features(state_in).astype(FULL) - mean0) * spread0
    d_own1 = own_features(grad0)
    d_own0 = d_own1.astype(FULL) + spread0 * (
        d_sum0 - extra0[0:1] - unit0 * extra0[1:2]
    )
    arrived = swap(
        jnp.where(
            first_core,
            jnp.concatenate([own1, d_own1]),
            jnp.concatenate([own0, d_own0.astype(LOW)]),
        )
    )

    def both_parts(low_value, high_value, arrived):
        mine = jnp.where(first_core, low_value, high_value)
        return jnp.concatenate(
            [jnp.where(first_core, mine, arrived), jnp.where(first_core, arrived, mine)], axis=1
        ).T[None]

    states_out = both_parts(own0, own1, arrived[:local])
    d_states_out = both_parts(d_own0, d_own1.astype(FULL), arrived[local:].astype(FULL))

    arrived = [
        swap(jnp.where(first_core, high, low)) for low, high in zip(all0, all1)
    ]
    g_down, g_out, g_up, g_qkv, b_down, b_out, b_up, b_qkv = finished(
        section,
        group,
        all0,
        all1,
        arrived,
        [
            down_weight.shape[1:],
            out_weight.shape[1:],
            up_weight.shape[1:],
            owns[0].shape,
        ],
        [(1, width), (1, width), (1, width), (3, local)],
    )
    return (
        states_out,
        d_states_out,
        g_qkv.swapaxes(1, 2)[None],
        b_qkv[None],
        g_out[None],
        b_out,
        g_up[None],
        b_up,
        g_down[None],
        b_down,
        norm_rows[0:2][None],
        norm_rows[2:4][None],
    )


def solution(mesh):
    in_specs = (
        P(DP, TENSOR),
        P(DP, TENSOR),
        P(DP, None),
        P(PIPE, None, None, TENSOR),
        P(PIPE, None, TENSOR),
        P(PIPE, TENSOR, None),
        P(PIPE, None),
        P(PIPE, None, TENSOR),
        P(PIPE, TENSOR),
        P(PIPE, TENSOR, None),
        P(PIPE, None),
        P(PIPE, None, None),
        P(PIPE, None, None),
    )
    out_specs = (
        P(PIPE, DP, TENSOR),
        P(PIPE, DP, TENSOR),
        P(PIPE, None, None, TENSOR),
        P(PIPE, None, TENSOR),
        P(PIPE, TENSOR, None),
        P(PIPE, None),
        P(PIPE, None, TENSOR),
        P(PIPE, TENSOR),
        P(PIPE, TENSOR, None),
        P(PIPE, None),
        P(PIPE, None, None),
        P(PIPE, None, None),
    )
    return jax.shard_map(body, mesh=mesh, in_specs=in_specs, out_specs=out_specs, check_vma=False)
```
